128 devices in a mesh: dp: 8 (over x, core), tensor: 16 (over y, z).
Axes of the slice: x: 4, y: 4, z: 4, core: 2. Of those that a mesh axis runs over, the one named last changes fastest.
Arguments:
- gradients: bfloat16 [8, 3, 2, 8192, 1024], P('dp', None, None, 'tensor'), may hold values from -60 to 60
- memory: bfloat16 [8, 3, 2, 8192, 1024], P('dp', None, None, 'tensor'), may hold values from -4 to 4
- initial_query: float32 [3, 2, 1024, 64], replicated, may hold values from -0.1875 to 0.1875
Outputs:
- new_memory: bfloat16 [8, 3, 2, 8192, 1024], P('dp', None, None, 'tensor')
- decompressed: bfloat16 [3, 2, 8192, 1024], P(None, None, 'tensor')
- updated_query_factor: float32 [3, 2, 1024, 64], replicated
The draws below stay inside these ranges and needn't reach their ends.
All inputs are finite; a program needn't handle non-finite values.
Results may differ from the reference program's by a relative error of at most 0.012.
Values may be sent and summed in bfloat16 or wider, within the bound.
A program may use at most 128 MiB of HBM per device.

```python
import jax
import jax.numpy as jnp
from jax import lax

D = 8192
KVW = 1024
R = 64
LAYERS = 3
REPLICAS = 8
N_DP = 8


def draw_gradients(key, part):
    key = jax.random.fold_in(key, 11)
    key_common, key_own, key_rows, key_cols = jax.random.split(key, 4)
    row_scale_factor = jnp.exp(jax.random.uniform(key_rows, (1, LAYERS, 2, D, 1), jnp.float32, -1.15, 1.15))
    col_scale = jnp.exp(jax.random.uniform(key_cols, (1, LAYERS, 2, 1, KVW), jnp.float32, -1.15, 1.15))
    common = jnp.clip(jax.random.normal(key_common, (1, LAYERS, 2, D, KVW), jnp.float32), -3.5, 3.5)
    own = jnp.clip(jax.random.normal(key_own, (REPLICAS, LAYERS, 2, D, KVW), jnp.float32), -3.5, 3.5)
    mixed = 0.55 * common + 0.85 * own
    return (mixed * row_scale_factor * col_scale).astype(jnp.bfloat16)


def shard_levels(stream_key, shape, cuts, least, largest):
    factor_of = 1.0
    for position, blocks in cuts:
        heights = jax.random.uniform(jax.random.fold_in(jax.random.fold_in(stream_key, 6), position), (blocks,), jnp.float32, least / len(cuts), largest / len(cuts))
        factor_of = factor_of * jnp.repeat(jnp.exp(heights), shape[position] // blocks).reshape((-1,) + (1,) * (len(shape) - 1 - position))
    return factor_of


def noise(rng, dims, spread, reach, pieces=(), kind=jnp.bfloat16):
    result = spread * jax.random.normal(rng, dims, jnp.float32)
    if pieces:
        result = result * shard_levels(rng, dims, pieces, -0.22, 0.18)
    return jnp.clip(result, -reach, reach).astype(kind)


def setup_inputs(seed: int = 0) -> dict:
    keys = jax.random.split(jax.random.key(seed), 4)
    return {
        "gradients": draw_gradients(jax.random.fold_in(keys[3], 71), 0),
        "memory": noise(keys[1], (REPLICAS, LAYERS, 2, D, KVW), 1.0, 4.0, ((0, 8), (3, 16))),
        "initial_query": noise(keys[2], (LAYERS, 2, KVW, R), KVW ** -0.5, 0.1875, (), jnp.float32),
    }


def orthonormal_basis(matrix_rows, gram_product):
    factor = jnp.linalg.cholesky(gram_product)
    return lax.linalg.triangular_solve(factor, matrix_rows, left_side=False, lower=True, transpose_a=True)

def reference(gradients, memory, initial_query):
    memory_blocks = []
    rebuilt_blocks = []
    query_factor_blocks = []
    for layer in range(LAYERS):
        mem_row = []
        reb_row = []
        qry_row = []
        for which in range(2):
            merged = (gradients[:, layer, which].astype(jnp.float32) + memory[:, layer, which].astype(jnp.float32)).astype(jnp.bfloat16)
            joined_wide_factor = merged.astype(jnp.float32)
            query_low = initial_query[layer, which].astype(jnp.bfloat16).astype(jnp.float32)
            summed = jnp.einsum('ndk,kr->dr', joined_wide_factor, query_low, precision=lax.Precision.HIGHEST)
            gram_product = jnp.dot(summed.T, summed, precision=lax.Precision.HIGHEST)
            basis = orthonormal_basis(summed, gram_product).astype(jnp.bfloat16)
            projected = jnp.einsum('ndk,dr->kr', joined_wide_factor, basis.astype(jnp.float32), precision=lax.Precision.HIGHEST)
            updated_query_factor = projected / N_DP
            query_next_low = updated_query_factor.astype(jnp.bfloat16)
            rebuilt = jnp.dot(basis.astype(jnp.float32), query_next_low.T.astype(jnp.float32), preferred_element_type=jnp.float32)
            mem_row.append((joined_wide_factor - rebuilt[None]).astype(jnp.bfloat16))
            reb_row.append(rebuilt.astype(jnp.bfloat16))
            qry_row.append(updated_query_factor)
        memory_blocks.append(jnp.stack(mem_row, axis=1))
        rebuilt_blocks.append(jnp.stack(reb_row, axis=0))
        query_factor_blocks.append(jnp.stack(qry_row, axis=0))
    return (jnp.stack(memory_blocks, axis=1), jnp.stack(rebuilt_blocks, axis=0), jnp.stack(query_factor_blocks, axis=0))
```

```python
import functools

import jax
import jax.numpy as jnp
from jax import lax
from jax.experimental import pallas as pl
from jax.experimental.pallas import tpu as pltpu
from jax.sharding import PartitionSpec as P

MESH = pl.DeviceIdType.MESH
F32 = jnp.float32
BF16 = jnp.bfloat16
LAYERS = 3
ROWS = 512
KVW = 1024
R = 64
NT = (((1,), (1,)), ((), ()))


def reduce_kernel(
    g_hbm, m_hbm, query_ref,
    merged, basis, w_all, linv,
    g_buf, m_buf, qpad, p_own, p_send, p_recv, x_slots, s_full, s_t,
    w_own, w_send, w_recv, w_sum, r1, s1, r2, e_slots, gram_y, gram_z, aug, linv_mine,
    load_sem, core_send, core_recv, x_send, x_recv, ax_send, ax_recv, gram_send, gram_recv,
):
    dp = lax.axis_index("dp")
    tensor = lax.axis_index("tensor")
    core = dp % 2
    coord = (dp // 2, tensor // 4, tensor % 4)

    def along(axis, k):
        c = [coord[0], coord[1], coord[2]]
        c[axis] = (c[axis] + k) % 4
        return (c[0] * 2 + core, c[1] * 4 + c[2])

    sibling = (dp + 1 - 2 * core, tensor)

    loads = []
    for l in range(LAYERS):
        for m in range(2):
            a = pltpu.make_async_copy(g_hbm.at[0, l, m], g_buf.at[l, m], load_sem.at[l, m, 0])
            b = pltpu.make_async_copy(m_hbm.at[0, l, m], m_buf.at[l, m], load_sem.at[l, m, 1])
            a.start()
            b.start()
            loads.append((a, b))

    barrier = pltpu.get_barrier_semaphore()
    pl.semaphore_signal(barrier, inc=1, device_id=sibling, device_id_type=MESH)
    for axis in range(3):
        for k in (1, 2, 3):
            pl.semaphore_signal(barrier, inc=1, device_id=along(axis, k), device_id_type=MESH)

    for l in range(LAYERS):
        for m in range(2):
            qpad[l, m, R * m:R * m + R, :] = query_ref[l, m].astype(BF16)
            qpad[l, m, R - R * m:2 * R - R * m, :] = jnp.zeros((R, KVW), BF16)

    sends = []

    def remote(src, dst, send_sem, recv_sem, device):
        c = pltpu.make_async_remote_copy(src, dst, send_sem, recv_sem, device_id=device, device_id_type=MESH)
        c.start()
        sends.append(c)
        return c

    half = ROWS // 2
    pc, xc, sc, wc = {}, {}, {}, {}

    def stage_a(l):
        total = None
        for m in range(2):
            a, b = loads[2 * l + m]
            a.wait()
            b.wait()
            merged[l, m] = (g_buf[l, m].astype(F32) + m_buf[l, m].astype(F32)).astype(BF16)
            part = lax.dot_general(merged[l, m], qpad[l, m], NT, preferred_element_type=F32)
            total = part if total is None else total + part
        p_own[l] = total
        p_send[l] = p_own[l, pl.ds(pl.multiple_of(half * (1 - core), half), half), :].astype(BF16)
        if l == 0:
            pl.semaphore_wait(barrier, 10)
        pc[l] = remote(p_send.at[l], p_recv.at[l], core_send.at[l, 0], core_recv.at[l, 0], sibling)

    def stage_b(l):
        pc[l].wait_recv()
        mine = p_own[l, pl.ds(pl.multiple_of(half * core, half), half), :] + p_recv[l].astype(F32)
        x_slots[l, coord[0]] = mine.astype(BF16)
        xc[l] = [
            remote(x_slots.at[l, coord[0]], x_slots.at[l, coord[0]], x_send.at[l, k - 1], x_recv.at[l, k - 1], along(0, k))
            for k in (1, 2, 3)
        ]

    def stage_c(l):
        for c in xc[l]:
            c.wait_recv()
        total = x_slots[l, 0].astype(F32)
        for j in (1, 2, 3):
            total = total + x_slots[l, j].astype(F32)
        s_full[l, core] = total.astype(BF16)
        sc[l] = remote(s_full.at[l, core], s_full.at[l, core], core_send.at[l, 1], core_recv.at[l, 1], sibling)

    def stage_d(l):
        sc[l].wait_recv()
        for h in range(2):
            s_t[l, :, half * h:half * h + half] = s_full[l, h].T
        other = s_t[l, pl.ds(pl.multiple_of(R * (1 - core), R), R), :]
        w = jnp.dot(other, merged[l, 1 - core], preferred_element_type=F32)
        for j in range(4):
            w_send[l, j] = w[:, 256 * j:256 * j + 256].astype(BF16)
        wc[l] = remote(w_send.at[l], w_recv.at[l], core_send.at[l, 2], core_recv.at[l, 2], sibling)
        mine = s_t[l, pl.ds(pl.multiple_of(R * core, R), R), :]
        w = jnp.dot(mine, merged[l, core], preferred_element_type=F32)
        for j in range(4):
            w_own[l, j] = w[:, 256 * j:256 * j + 256]

    def spread(l, phase, axis, source, target):
        return [
            remote(source((coord[axis] + k) % 4), target(k), ax_send.at[l, phase, k - 1], ax_recv.at[l, phase, k - 1], along(axis, k))
            for k in (1, 2, 3)
        ]

    ac = {}

    def axes(l):
        return l % 3, (l + 1) % 3, (l + 2) % 3

    def stage_e(l):
        wc[l].wait_recv()
        w_sum[l] = (w_own[l] + w_recv[l].astype(F32)).astype(BF16)
        ac[l, 0] = spread(l, 0, axes(l)[0], lambda j: w_sum.at[l, j], lambda k: r1.at[l, k - 1])

    def row16(j):
        return pl.ds(pl.multiple_of(j * 16, 16), 16)

    def stage_f(l):
        for c in ac[l, 0]:
            c.wait_recv()
        total = w_sum[l, coord[axes(l)[0]]].astype(F32)
        for k in range(3):
            total = total + r1[l, k].astype(F32)
        s1[l] = total.astype(BF16)
        ac[l, 1] = spread(l, 1, axes(l)[1], lambda j: s1.at[l, row16(j)], lambda k: r2.at[l, k - 1])

    def stage_h(l):
        for c in ac[l, 1]:
            c.wait_recv()
        total = s1[l, row16(coord[axes(l)[1]]), :].astype(F32)
        for k in range(3):
            total = total + r2[l, k].astype(F32)
        mine = coord[axes(l)[2]]
        e_slots[l, mine] = total.astype(BF16)
        ac[l, 2] = spread(l, 2, axes(l)[2], lambda j: e_slots.at[l, mine], lambda k: e_slots.at[l, mine])

    def stage_i(l):
        for c in ac[l, 2]:
            c.wait_recv()
        total = e_slots[l, 0].astype(F32)
        for j in (1, 2, 3):
            total = total + e_slots[l, j].astype(F32)
        a0, a1 = coord[axes(l)[0]], coord[axes(l)[1]]
        w_all[l, core, a0, row16(a1), :] = total.astype(BF16)
        piece = w_all.at[l, core, a0, row16(a1)]
        ac[l, 3] = spread(l, 3, axes(l)[1], lambda j: piece, lambda k: piece)

    def stage_j(l):
        for c in ac[l, 3]:
            c.wait_recv()
        piece = w_all.at[l, core, coord[axes(l)[0]]]
        ac[l, 4] = spread(l, 4, axes(l)[0], lambda j: piece, lambda k: piece)

    def stage_k(l):
        for c in ac[l, 4]:
            c.wait_recv()
        ac[l, 5] = remote(w_all.at[l, core], w_all.at[l, core], core_send.at[l, 3], core_recv.at[l, 3], sibling)

    gc = {}

    def gram_a():
        grams = []
        for l in range(LAYERS):
            mine = s_t[l, pl.ds(pl.multiple_of(R * core, R), R), :]
            grams.append(lax.dot_general(mine, mine, NT, preferred_element_type=F32))
        slot = coord[1]
        gram_y[slot, 0:64, :] = jnp.concatenate([grams[0], grams[1]], axis=1)
        gram_y[slot, 64:96, :] = jnp.concatenate([grams[2][0:32], grams[2][32:64]], axis=1)
        gc[0] = [
            remote(gram_y.at[slot], gram_y.at[slot], gram_send.at[0, k - 1], gram_recv.at[0, k - 1], along(1, k)) for k in (1, 2, 3)
        ]

    def gram_b():
        for c in gc[0]:
            c.wait_recv()
        slot = coord[2]
        gram_z[slot] = ((gram_y[0] + gram_y[1]) + gram_y[2]) + gram_y[3]
        gc[1] = [
            remote(gram_z.at[slot], gram_z.at[slot], gram_send.at[1, k - 1], gram_recv.at[1, k - 1], along(2, k)) for k in (1, 2, 3)
        ]

    def gram_c():
        for c in gc[1]:
            c.wait_recv()
        total = ((gram_z[0] + gram_z[1]) + gram_z[2]) + gram_z[3]
        lane = lax.broadcasted_iota(jnp.int32, (R, 2 * R), 1)
        row = lax.broadcasted_iota(jnp.int32, (R, 2 * R), 0)
        eye = (lane == row + R).astype(F32)
        both, last = total[0:64], total[64:96]
        aug[0] = jnp.where(lane < R, both, eye)
        aug[1] = jnp.where(lane < R, pltpu.roll(both, R, 1), eye)
        aug[2] = jnp.where(lane < R, jnp.concatenate([last, pltpu.roll(last, R, 1)], axis=0), eye)

        def step(b, carry):
            for i in range(8):
                j = b * 8 + i
                for l in range(LAYERS):
                    pivot_row = aug[l, pl.ds(j, 1), :]
                    scaled = pivot_row / pivot_row[:, i:i + 1]
                    a = aug[l]
                    aug[l] = a - jnp.where(row > j, a[:, i:i + 1], 0.0) * scaled
            for l in range(LAYERS):
                aug[l] = pltpu.roll(aug[l], 2 * R - 8, 1)
            return carry

        lax.fori_loop(0, R // 8, step, 0)
        for l in range(LAYERS):
            a = aug[l]
            pivots = jnp.sum(jnp.where(lane == row + R, a, 0.0), axis=1, keepdims=True)
            linv[l, core] = jnp.where(lane < R, a * lax.rsqrt(pivots), 0.0)
        gc[2] = [
            remote(linv.at[l, core], linv.at[l, core], core_send.at[l, 4], core_recv.at[l, 4], sibling) for l in range(LAYERS)
        ]

    def gram_d():
        for l in range(LAYERS):
            gc[2][l].wait_recv()
        for l in range(LAYERS):
            block = jnp.concatenate([linv[l, 0], pltpu.roll(linv[l, 1], R, 1)], axis=0)
            high = block.astype(BF16)
            low = (block - high.astype(F32)).astype(BF16)
            for h in range(2):
                s = s_full[l, h]
                out = lax.dot_general(s, high, NT, preferred_element_type=F32)
                out = out + lax.dot_general(s, low, NT, preferred_element_type=F32)
                basis[l, half * h:half * h + half, :] = out.astype(BF16)

    stage_a(0)
    stage_a(1)
    stage_b(0)
    stage_a(2)
    stage_b(1)
    stage_b(2)
    stage_c(0)
    stage_c(1)
    stage_d(0)
    stage_c(2)
    stage_d(1)
    stage_e(0)
    stage_d(2)
    stage_e(1)
    stage_e(2)
    gram_a()
    for l in range(LAYERS):
        stage_f(l)
    gram_b()
    for l in range(LAYERS):
        stage_h(l)
    gram_c()
    for l in range(LAYERS):
        stage_i(l)
    gram_d()
    for l in range(LAYERS):
        stage_j(l)
    for l in range(LAYERS):
        stage_k(l)
    for l in range(LAYERS):
        ac[l, 5].wait_recv()
    for c in sends:
        c.wait_send()


def rebuild_kernel(replicas, merged, basis, w_all, linv, memory_out, rebuilt_out, query_out, qpad):
    m = pl.program_id(1)
    block = pl.program_id(2)

    @pl.when(block == 0)
    def _():
        inverse = linv[0, 0][:, 0:R]
        high = inverse.astype(BF16)
        low = (inverse - high.astype(F32)).astype(BF16)
        qpad[pl.ds(pl.multiple_of(R - R * m, R), R), :] = jnp.zeros((R, KVW), BF16)
        for j in range(4):
            w = w_all[0, 0, j]
            q = jnp.dot(high, w, preferred_element_type=F32) + jnp.dot(low, w, preferred_element_type=F32)
            q = q * (1.0 / replicas)
            query_out[0, 0, :, 256 * j:256 * j + 256] = q
            qpad[pl.ds(pl.multiple_of(R * m, R), R), 256 * j:256 * j + 256] = q.astype(BF16)

    rebuilt = jnp.dot(basis[0], qpad[...], preferred_element_type=F32)
    rebuilt_out[0, 0] = rebuilt.astype(BF16)
    memory_out[0, 0, 0] = (merged[0, 0].astype(F32) - rebuilt).astype(BF16)


def body(gradients, memory, initial_query):
    replicas = lax.axis_size("dp")
    vmem = pl.BlockSpec(memory_space=pltpu.VMEM)
    hbm = pl.BlockSpec(memory_space=pl.ANY)
    query_t = jnp.swapaxes(initial_query, 2, 3)
    half = ROWS // 2
    dma = pltpu.SemaphoreType.DMA
    merged, basis, w_all, linv = pl.pallas_call(
        reduce_kernel,
        name="reduce",
        out_shape=[
            pltpu.VMEM((LAYERS, 2, ROWS, KVW), BF16),
            pltpu.VMEM((LAYERS, ROWS, 2 * R), BF16),
            pltpu.VMEM((LAYERS, 2, 4, R, 256), BF16),
            pltpu.VMEM((LAYERS, 2, R, 2 * R), F32),
        ],
        in_specs=[hbm, hbm, vmem],
        out_specs=[vmem] * 4,
        scratch_shapes=[
            pltpu.VMEM((LAYERS, 2, ROWS, KVW), BF16),
            pltpu.VMEM((LAYERS, 2, ROWS, KVW), BF16),
            pltpu.VMEM((LAYERS, 2, 2 * R, KVW), BF16),
            pltpu.VMEM((LAYERS, ROWS, 2 * R), F32),
            pltpu.VMEM((LAYERS, half, 2 * R), BF16),
            pltpu.VMEM((LAYERS, half, 2 * R), BF16),
            pltpu.VMEM((LAYERS, 4, half, 2 * R), BF16),
            pltpu.VMEM((LAYERS, 2, half, 2 * R), BF16),
            pltpu.VMEM((LAYERS, 2 * R, ROWS), BF16),
            pltpu.VMEM((LAYERS, 4, R, 256), F32),
            pltpu.VMEM((LAYERS, 4, R, 256), BF16),
            pltpu.VMEM((LAYERS, 4, R, 256), BF16),
            pltpu.VMEM((LAYERS, 4, R, 256), BF16),
            pltpu.VMEM((LAYERS, 3, R, 256), BF16),
            pltpu.VMEM((LAYERS, R, 256), BF16),
            pltpu.VMEM((LAYERS, 3, 16, 256), BF16),
            pltpu.VMEM((LAYERS, 4, 16, 256), BF16),
            pltpu.VMEM((4, 96, 2 * R), F32),
            pltpu.VMEM((4, 96, 2 * R), F32),
            pltpu.VMEM((LAYERS, R, 2 * R), F32),
            pltpu.VMEM((8, 128), F32),
            dma((LAYERS, 2, 2)),
            dma((LAYERS, 5)),
            dma((LAYERS, 5)),
            dma((LAYERS, 3)),
            dma((LAYERS, 3)),
            dma((LAYERS, 5, 3)),
            dma((LAYERS, 5, 3)),
            dma((2, 3)),
            dma((2, 3)),
        ],
        compiler_params=pltpu.CompilerParams(collective_id=0, has_side_effects=True, vmem_limit_bytes=40 << 20),
    )(gradients, memory, query_t)

    blocks = 2
    rows = ROWS // blocks
    new_memory, rebuilt, query = pl.pallas_call(
        functools.partial(rebuild_kernel, replicas),
        name="rebuild",
        grid=(LAYERS, 2, blocks),
        out_shape=[
            jax.ShapeDtypeStruct((1, LAYERS, 2, ROWS, KVW), BF16),
            jax.ShapeDtypeStruct((LAYERS, 2, ROWS, KVW), BF16),
            jax.ShapeDtypeStruct((LAYERS, 2, R, KVW), F32),
        ],
        in_specs=[
            pl.BlockSpec((1, 1, rows, KVW), lambda l, m, b: (l, m, b, 0)),
            pl.BlockSpec((1, rows, 2 * R), lambda l, m, b: (l, b, 0)),
            pl.BlockSpec((1, 1, 4, R, 256), lambda l, m, b: (l, m, 0, 0, 0)),
            pl.BlockSpec((1, 1, R, 2 * R), lambda l, m, b: (l, m, 0, 0)),
        ],
        out_specs=[
            pl.BlockSpec((1, 1, 1, rows, KVW), lambda l, m, b: (0, l, m, b, 0)),
            pl.BlockSpec((1, 1, rows, KVW), lambda l, m, b: (l, m, b, 0)),
            pl.BlockSpec((1, 1, R, KVW), lambda l, m, b: (l, m, 0, 0)),
        ],
        scratch_shapes=[pltpu.VMEM((2 * R, KVW), BF16)],
        compiler_params=pltpu.CompilerParams(vmem_limit_bytes=20 << 20),
    )(merged, basis, w_all, linv)
    return new_memory, rebuilt, jnp.swapaxes(query, 2, 3)


def solution(mesh):
    in_specs = (P("dp", None, None, "tensor", None), P("dp", None, None, "tensor", None), P())
    out_specs = (P("dp", None, None, "tensor", None), P(None, None, "tensor", None), P())
    return jax.shard_map(body, mesh=mesh, in_specs=in_specs, out_specs=out_specs, check_vma=False)
```

```python
import functools

import jax
import jax.numpy as jnp
from jax import lax
from jax.experimental import pallas as pl
from jax.experimental.pallas import tpu as pltpu
from jax.sharding import PartitionSpec as P

MESH = pl.DeviceIdType.MESH
F32 = jnp.float32
BF16 = jnp.bfloat16
LAYERS = 3
ROWS = 512
KVW = 1024
R = 64
CHUNK = 256
NT = (((1,), (1,)), ((), ()))


def reduce_kernel(
    g_hbm, m_hbm, query_hbm,
    merged, basis, w_all, linv,
    g_buf, m_buf, query, qpad, p_own, p_send, p_recv, x_slots, s_full, s_t,
    w_own, w_send, w_recv, w_sum, r1, s1, r2, e_slots, gram_y, gram_z,
    load_sem, query_sem, core_send, core_recv, x_send, x_recv, ax_send, ax_recv, gram_send, gram_recv,
):
    dp = lax.axis_index("dp")
    tensor = lax.axis_index("tensor")
    core = dp % 2
    coord = (dp // 2, tensor // 4, tensor % 4)

    def along(axis, k):
        c = [coord[0], coord[1], coord[2]]
        c[axis] = (c[axis] + k) % 4
        return (c[0] * 2 + core, c[1] * 4 + c[2])

    sibling = (dp + 1 - 2 * core, tensor)

    query_load = pltpu.make_async_copy(query_hbm, query, query_sem)
    query_load.start()
    loads = []
    for l in range(LAYERS):
        for m in range(2):
            a = pltpu.make_async_copy(g_hbm.at[0, l, m], g_buf.at[l, m], load_sem.at[l, m, 0])
            b = pltpu.make_async_copy(m_hbm.at[0, l, m], m_buf.at[l, m], load_sem.at[l, m, 1])
            a.start()
            b.start()
            loads.append((a, b))

    barrier = pltpu.get_barrier_semaphore()
    pl.semaphore_signal(barrier, inc=1, device_id=sibling, device_id_type=MESH)
    for axis in range(3):
        for k in (1, 2, 3):
            pl.semaphore_signal(barrier, inc=1, device_id=along(axis, k), device_id_type=MESH)

    query_load.wait()
    column = lax.broadcasted_iota(jnp.int32, (KVW, 2 * R), 1)
    for l in range(LAYERS):
        pair = jnp.concatenate([query[l, 0], query[l, 1]], axis=0).astype(BF16).T
        for m in range(2):
            qpad[l, m] = jnp.where((column >= R * m) & (column < R * m + R), pair, jnp.zeros_like(pair))

    sends = []

    def remote(src, dst, send_sem, recv_sem, device):
        c = pltpu.make_async_remote_copy(src, dst, send_sem, recv_sem, device_id=device, device_id_type=MESH)
        c.start()
        sends.append(c)
        return c

    half = ROWS // 2
    pc, xc, sc, wc = {}, {}, {}, {}

    def stage_a(l):
        for m in range(2):
            a, b = loads[2 * l + m]
            a.wait()
            b.wait()
            for r in range(0, ROWS, CHUNK):
                rows = slice(r, r + CHUNK)
                block = g_buf[l, m, rows] + m_buf[l, m, rows]
                merged[l, m, rows] = block
                part = jnp.dot(block, qpad[l, m], preferred_element_type=F32)
                p_own[l, rows] = part if m == 0 else p_own[l, rows] + part
        p_send[l] = p_own[l, pl.ds(pl.multiple_of(half * (1 - core), half), half), :].astype(BF16)
        if l == 0:
            pl.semaphore_wait(barrier, 10)
        pc[l] = remote(p_send.at[l], p_recv.at[l], core_send.at[l, 0], core_recv.at[l, 0], sibling)

    def stage_b(l):
        pc[l].wait_recv()
        mine = p_own[l, pl.ds(pl.multiple_of(half * core, half), half), :] + p_recv[l].astype(F32)
        x_slots[l, coord[0]] = mine.astype(BF16)
        xc[l] = [
            remote(x_slots.at[l, coord[0]], x_slots.at[l, coord[0]], x_send.at[l, k - 1], x_recv.at[l, k - 1], along(0, k))
            for k in (1, 2, 3)
        ]

    def stage_c(l):
        for c in xc[l]:
            c.wait_recv()
        total = x_slots[l, 0].astype(F32)
        for j in (1, 2, 3):
            total = total + x_slots[l, j].astype(F32)
        s_full[l, core] = total.astype(BF16)
        sc[l] = remote(s_full.at[l, core], s_full.at[l, core], core_send.at[l, 1], core_recv.at[l, 1], sibling)

    def stage_d(l):
        sc[l].wait_recv()
        for h in range(2):
            s_t[l, :, half * h:half * h + half] = s_full[l, h].T
        other = s_t[l, pl.ds(pl.multiple_of(R * (1 - core), R), R), :]
        w = jnp.dot(other, merged[l, 1 - core], preferred_element_type=F32)
        for j in range(4):
            w_send[l, j] = w[:, 256 * j:256 * j + 256].astype(BF16)
        wc[l] = remote(w_send.at[l], w_recv.at[l], core_send.at[l, 2], core_recv.at[l, 2], sibling)
        mine = s_t[l, pl.ds(pl.multiple_of(R * core, R), R), :]
        w = jnp.dot(mine, merged[l, core], preferred_element_type=F32)
        for j in range(4):
            w_own[l, j] = w[:, 256 * j:256 * j + 256]

    def spread(l, phase, axis, source, target):
        return [
            remote(source((coord[axis] + k) % 4), target(k), ax_send.at[l, phase, k - 1], ax_recv.at[l, phase, k - 1], along(axis, k))
            for k in (1, 2, 3)
        ]

    ac = {}

    def axes(l):
        return l % 3, (l + 1) % 3, (l + 2) % 3

    def stage_e(l):
        wc[l].wait_recv()
        w_sum[l] = (w_own[l] + w_recv[l].astype(F32)).astype(BF16)
        ac[l, 0] = spread(l, 0, axes(l)[0], lambda j: w_sum.at[l, j], lambda k: r1.at[l, k - 1])

    def row16(j):
        return pl.ds(pl.multiple_of(j * 16, 16), 16)

    def stage_f(l):
        for c in ac[l, 0]:
            c.wait_recv()
        total = w_sum[l, coord[axes(l)[0]]].astype(F32)
        for k in range(3):
            total = total + r1[l, k].astype(F32)
        s1[l] = total.astype(BF16)
        ac[l, 1] = spread(l, 1, axes(l)[1], lambda j: s1.at[l, row16(j)], lambda k: r2.at[l, k - 1])

    def stage_h(l):
        for c in ac[l, 1]:
            c.wait_recv()
        total = s1[l, row16(coord[axes(l)[1]]), :].astype(F32)
        for k in range(3):
            total = total + r2[l, k].astype(F32)
        mine = coord[axes(l)[2]]
        e_slots[l, mine] = total.astype(BF16)
        ac[l, 2] = spread(l, 2, axes(l)[2], lambda j: e_slots.at[l, mine], lambda k: e_slots.at[l, mine])

    def stage_i(l):
        for c in ac[l, 2]:
            c.wait_recv()
        total = e_slots[l, 0].astype(F32)
        for j in (1, 2, 3):
            total = total + e_slots[l, j].astype(F32)
        a0, a1 = coord[axes(l)[0]], coord[axes(l)[1]]
        w_all[l, core, a0, row16(a1), :] = total.astype(BF16)
        piece = w_all.at[l, core, a0, row16(a1)]
        ac[l, 3] = spread(l, 3, axes(l)[1], lambda j: piece, lambda k: piece)

    def stage_j(l):
        for c in ac[l, 3]:
            c.wait_recv()
        piece = w_all.at[l, core, coord[axes(l)[0]]]
        ac[l, 4] = spread(l, 4, axes(l)[0], lambda j: piece, lambda k: piece)

    def stage_k(l):
        for c in ac[l, 4]:
            c.wait_recv()
        ac[l, 5] = remote(w_all.at[l, core], w_all.at[l, core], core_send.at[l, 3], core_recv.at[l, 3], sibling)

    gc = {}

    def gram_a():
        grams = []
        for l in range(LAYERS):
            mine = s_t[l, pl.ds(pl.multiple_of(R * core, R), R), :]
            grams.append(lax.dot_general(mine, mine, NT, preferred_element_type=F32))
        slot = coord[1]
        gram_y[slot, 0:64, :] = jnp.concatenate([grams[0], grams[1]], axis=1)
        gram_y[slot, 64:96, :] = jnp.concatenate([grams[2][0:32], grams[2][32:64]], axis=1)
        gc[0] = [
            remote(gram_y.at[slot], gram_y.at[slot], gram_send.at[0, k - 1], gram_recv.at[0, k - 1], along(1, k)) for k in (1, 2, 3)
        ]

    def gram_b():
        for c in gc[0]:
            c.wait_recv()
        slot = coord[2]
        gram_z[slot] = ((gram_y[0] + gram_y[1]) + gram_y[2]) + gram_y[3]
        gc[1] = [
            remote(gram_z.at[slot], gram_z.at[slot], gram_send.at[1, k - 1], gram_recv.at[1, k - 1], along(2, k)) for k in (1, 2, 3)
        ]

    def gram_c():
        for c in gc[1]:
            c.wait_recv()
        total = ((gram_z[0] + gram_z[1]) + gram_z[2]) + gram_z[3]
        lane = lax.broadcasted_iota(jnp.int32, (R, 2 * R), 1)
        row = lax.broadcasted_iota(jnp.int32, (R, 2 * R), 0)
        eye = (lane == row + R).astype(F32)
        both, last = total[0:64], total[64:96]
        start = (
            jnp.where(lane < R, both, eye),
            jnp.where(lane < R, pltpu.roll(both, R, 1), eye),
            jnp.where(lane < R, jnp.concatenate([last, pltpu.roll(last, R, 1)], axis=0), eye),
        )

        def step(b, carry):
            left = row < R - 8 * b
            state = list(carry)
            for i in range(8):
                below = left & (row > i)
                for l in range(LAYERS):
                    a = state[l]
                    scaled = a[i:i + 1, :] / a[i:i + 1, i:i + 1]
                    state[l] = a - jnp.where(below, a[:, i:i + 1], 0.0) * scaled
            return tuple(pltpu.roll(jnp.concatenate([a[8:], a[:8]], axis=0), 2 * R - 8, 1) for a in state)

        done = lax.fori_loop(0, R // 8, step, start)
        for l in range(LAYERS):
            a = done[l]
            pivots = jnp.sum(jnp.where(lane == row + R, a, 0.0), axis=1, keepdims=True)
            linv[l, core] = jnp.where(lane < R, a * lax.rsqrt(pivots), 0.0)
        gc[2] = [
            remote(linv.at[l, core], linv.at[l, core], core_send.at[l, 4], core_recv.at[l, 4], sibling) for l in range(LAYERS)
        ]

    def gram_d():
        for l in range(LAYERS):
            gc[2][l].wait_recv()
        for l in range(LAYERS):
            block = jnp.concatenate([linv[l, 0], pltpu.roll(linv[l, 1], R, 1)], axis=0)
            high = block.astype(BF16)
            low = (block - high.astype(F32)).astype(BF16)
            for h in range(2):
                s = s_full[l, h]
                out = lax.dot_general(s, high, NT, preferred_element_type=F32)
                out = out + lax.dot_general(s, low, NT, preferred_element_type=F32)
                basis[l, half * h:half * h + half, :] = out.astype(BF16)

    plan = [
        (stage_a, 0), (stage_a, 1), (stage_b, 0), (stage_a, 2), (stage_b, 1), (stage_b, 2),
        (stage_c, 0), (stage_c, 1), (stage_d, 0), (stage_c, 2), (stage_d, 1), (stage_e, 0), (stage_d, 2), (stage_e, 1), (stage_e, 2),
        (gram_a,), (stage_f, 0), (stage_f, 1), (stage_f, 2), (gram_b,), (stage_h, 0), (stage_h, 1), (stage_h, 2), (gram_c,),
        (stage_i, 0), (stage_i, 1), (stage_i, 2), (gram_d,), (stage_j, 0), (stage_j, 1), (stage_j, 2),
        (stage_k, 0), (stage_k, 1), (stage_k, 2),
    ]
    for stage in plan:
        stage[0](*stage[1:])
    for l in range(LAYERS):
        ac[l, 5].wait_recv()
    for c in sends:
        c.wait_send()


def rebuild_kernel(
    replicas, merged, basis, w_all, linv, memory_out, rebuilt_out, query_out, qpad, memory_buf, rebuilt_buf, query_buf, sem, query_sem
):
    copies = []

    def write(src, dst, s):
        c = pltpu.make_async_copy(src, dst, s)
        c.start()
        copies.append(c)

    for l in range(LAYERS):
        for m in range(2):
            inverse = linv[l, m][:, 0:R]
            high = inverse.astype(BF16)
            low = (inverse - high.astype(F32)).astype(BF16)
            qpad[l, m, R - R * m:2 * R - R * m, :] = jnp.zeros((R, KVW), BF16)
            for j in range(4):
                w = w_all[l, m, j]
                q = jnp.dot(high, w, preferred_element_type=F32) + jnp.dot(low, w, preferred_element_type=F32)
                q = q * (1.0 / replicas)
                query_buf[l, m, :, 256 * j:256 * j + 256] = q
                qpad[l, m, R * m:R * m + R, 256 * j:256 * j + 256] = q.astype(BF16)
            write(query_buf.at[l, m], query_out.at[l, m], query_sem.at[l, m])
            for n, r in enumerate(range(0, ROWS, CHUNK)):
                rows = slice(r, r + CHUNK)
                at = pl.ds(r, CHUNK)
                rebuilt = jnp.dot(basis[l, rows], qpad[l, m], preferred_element_type=F32)
                rebuilt_buf[l, m, rows] = rebuilt.astype(BF16)
                memory_buf[l, m, rows] = (merged[l, m, rows].astype(F32) - rebuilt).astype(BF16)
                write(rebuilt_buf.at[l, m, at], rebuilt_out.at[l, m, at], sem.at[l, m, n, 0])
                write(memory_buf.at[l, m, at], memory_out.at[0, l, m, at], sem.at[l, m, n, 1])
    for c in copies:
        c.wait()


def body(gradients, memory, initial_query):
    replicas = lax.axis_size("dp")
    vmem = pl.BlockSpec(memory_space=pltpu.VMEM)
    hbm = pl.BlockSpec(memory_space=pltpu.HBM)
    query_t = jnp.swapaxes(initial_query, 2, 3)
    half = ROWS // 2
    dma = pltpu.SemaphoreType.DMA
    merged, basis, w_all, linv = pl.pallas_call(
        reduce_kernel,
        name="reduce",
        out_shape=[
            pltpu.VMEM((LAYERS, 2, ROWS, KVW), BF16),
            pltpu.VMEM((LAYERS, ROWS, 2 * R), BF16),
            pltpu.VMEM((LAYERS, 2, 4, R, 256), BF16),
            pltpu.VMEM((LAYERS, 2, R, 2 * R), F32),
        ],
        in_specs=[hbm, hbm, hbm],
        out_specs=[vmem] * 4,
        scratch_shapes=[
            pltpu.VMEM((LAYERS, 2, ROWS, KVW), BF16),
            pltpu.VMEM((LAYERS, 2, ROWS, KVW), BF16),
            pltpu.VMEM((LAYERS, 2, R, KVW), F32),
            pltpu.VMEM((LAYERS, 2, KVW, 2 * R), BF16),
            pltpu.VMEM((LAYERS, ROWS, 2 * R), F32),
            pltpu.VMEM((LAYERS, half, 2 * R), BF16),
            pltpu.VMEM((LAYERS, half, 2 * R), BF16),
            pltpu.VMEM((LAYERS, 4, half, 2 * R), BF16),
            pltpu.VMEM((LAYERS, 2, half, 2 * R), BF16),
            pltpu.VMEM((LAYERS, 2 * R, ROWS), BF16),
            pltpu.VMEM((LAYERS, 4, R, 256), F32),
            pltpu.VMEM((LAYERS, 4, R, 256), BF16),
            pltpu.VMEM((LAYERS, 4, R, 256), BF16),
            pltpu.VMEM((LAYERS, 4, R, 256), BF16),
            pltpu.VMEM((LAYERS, 3, R, 256), BF16),
            pltpu.VMEM((LAYERS, R, 256), BF16),
            pltpu.VMEM((LAYERS, 3, 16, 256), BF16),
            pltpu.VMEM((LAYERS, 4, 16, 256), BF16),
            pltpu.VMEM((4, 96, 2 * R), F32),
            pltpu.VMEM((4, 96, 2 * R), F32),
            dma((LAYERS, 2, 2)),
            dma,
            dma((LAYERS, 5)),
            dma((LAYERS, 5)),
            dma((LAYERS, 3)),
            dma((LAYERS, 3)),
            dma((LAYERS, 5, 3)),
            dma((LAYERS, 5, 3)),
            dma((2, 3)),
            dma((2, 3)),
        ],
        compiler_params=pltpu.CompilerParams(collective_id=0, has_side_effects=True, vmem_limit_bytes=54 << 20),
    )(gradients, memory, query_t)

    new_memory, rebuilt, query = pl.pallas_call(
        functools.partial(rebuild_kernel, replicas),
        name="rebuild",
        out_shape=[
            jax.ShapeDtypeStruct((1, LAYERS, 2, ROWS, KVW), BF16),
            jax.ShapeDtypeStruct((LAYERS, 2, ROWS, KVW), BF16),
            jax.ShapeDtypeStruct((LAYERS, 2, R, KVW), F32),
        ],
        in_specs=[vmem] * 4,
        out_specs=[hbm] * 3,
        scratch_shapes=[
            pltpu.VMEM((LAYERS, 2, 2 * R, KVW), BF16),
            pltpu.VMEM((LAYERS, 2, ROWS, KVW), BF16),
            pltpu.VMEM((LAYERS, 2, ROWS, KVW), BF16),
            pltpu.VMEM((LAYERS, 2, R, KVW), F32),
            dma((LAYERS, 2, ROWS // CHUNK, 2)),
            dma((LAYERS, 2)),
        ],
        compiler_params=pltpu.CompilerParams(vmem_limit_bytes=36 << 20),
    )(merged, basis, w_all, linv)
    return new_memory, rebuilt, jnp.swapaxes(query, 2, 3)


def solution(mesh):
    in_specs = (P("dp", None, None, "tensor", None), P("dp", None, None, "tensor", None), P())
    out_specs = (P("dp", None, None, "tensor", None), P(None, None, "tensor", None), P())
    return jax.shard_map(body, mesh=mesh, in_specs=in_specs, out_specs=out_specs, check_vma=False)
```

```python
import functools

import jax
import jax.numpy as jnp
from jax import lax
from jax.experimental import pallas as pl
from jax.experimental.pallas import tpu as pltpu
from jax.sharding import PartitionSpec as P

MESH = pl.DeviceIdType.MESH
F32 = jnp.float32
BF16 = jnp.bfloat16
LAYERS = 3
ROWS = 512
KVW = 1024
R = 64
CHUNK = 256
DEPTH = 3
NT = (((1,), (1,)), ((), ()))


def reduce_kernel(
    g_hbm, m_hbm, query_hbm,
    merged, basis, w_all, linv,
    g_buf, m_buf, query, qpad, p_own, p_send, p_recv, x_slots, s_full, s_t,
    w_own, w_send, w_recv, w_sum, r1, e1, e2, gram_y, gram_z, aug,
    load_sem, query_sem, core_send, core_recv, x_send, x_recv, ax_send, ax_recv, gram_send, gram_recv,
):
    dp = lax.axis_index("dp")
    tensor = lax.axis_index("tensor")
    core = dp % 2
    coord = (dp // 2, tensor // 4, tensor % 4)

    def along(axis, k):
        c = [coord[0], coord[1], coord[2]]
        c[axis] = (c[axis] + k) % 4
        return (c[0] * 2 + core, c[1] * 4 + c[2])

    sibling = (dp + 1 - 2 * core, tensor)

    query_loads = [pltpu.make_async_copy(query_hbm.at[l], query.at[l], query_sem.at[l]) for l in range(LAYERS)]
    loads = [
        (
            pltpu.make_async_copy(g_hbm.at[0, l, m], g_buf.at[l, m], load_sem.at[l, m, 0]),
            pltpu.make_async_copy(m_hbm.at[0, l, m], m_buf.at[l, m], load_sem.at[l, m, 1]),
        )
        for l in range(LAYERS)
        for m in range(2)
    ]

    def load(i):
        if i % 2 == 0:
            query_loads[i // 2].start()
        loads[i][0].start()
        loads[i][1].start()

    for i in range(DEPTH):
        load(i)

    barrier = pltpu.get_barrier_semaphore()
    pl.semaphore_signal(barrier, inc=1, device_id=sibling, device_id_type=MESH)
    for axis in range(3):
        for k in (1, 2, 3):
            pl.semaphore_signal(barrier, inc=1, device_id=along(axis, k), device_id_type=MESH)

    column = lax.broadcasted_iota(jnp.int32, (KVW, 2 * R), 1)

    def right_factor(l):
        query_loads[l].wait()
        pair = jnp.concatenate([query[l, 0], query[l, 1]], axis=0).astype(BF16).T
        for m in range(2):
            qpad[l, m] = jnp.where((column >= R * m) & (column < R * m + R), pair, jnp.zeros_like(pair))

    sends = []

    def remote(src, dst, send_sem, recv_sem, device):
        c = pltpu.make_async_remote_copy(src, dst, send_sem, recv_sem, device_id=device, device_id_type=MESH)
        c.start()
        sends.append(c)
        return c

    half = ROWS // 2
    pc, xc, sc, wc = {}, {}, {}, {}

    def stage_a(l):
        right_factor(l)
        for m in range(2):
            i = 2 * l + m
            loads[i][0].wait()
            loads[i][1].wait()
            if i + DEPTH < len(loads):
                load(i + DEPTH)
            for r in range(0, ROWS, CHUNK):
                rows = slice(r, r + CHUNK)
                block = g_buf[l, m, rows] + m_buf[l, m, rows]
                merged[l, m, rows] = block
                part = jnp.dot(block, qpad[l, m], preferred_element_type=F32)
                p_own[l, rows] = part if m == 0 else p_own[l, rows] + part
        p_send[l] = p_own[l, pl.ds(pl.multiple_of(half * (1 - core), half), half), :].astype(BF16)
        if l == 0:
            pl.semaphore_wait(barrier, 10)
        pc[l] = remote(p_send.at[l], p_recv.at[l], core_send.at[l, 0], core_recv.at[l, 0], sibling)

    def stage_b(l):
        pc[l].wait_recv()
        mine = p_own[l, pl.ds(pl.multiple_of(half * core, half), half), :] + p_recv[l].astype(F32)
        x_slots[l, coord[0]] = mine.astype(BF16)
        xc[l] = [
            remote(x_slots.at[l, coord[0]], x_slots.at[l, coord[0]], x_send.at[l, k - 1], x_recv.at[l, k - 1], along(0, k))
            for k in (1, 2, 3)
        ]

    def stage_c(l):
        for c in xc[l]:
            c.wait_recv()
        total = x_slots[l, 0].astype(F32)
        for j in (1, 2, 3):
            total = total + x_slots[l, j].astype(F32)
        s_full[l, core] = total.astype(BF16)
        sc[l] = remote(s_full.at[l, core], s_full.at[l, core], core_send.at[l, 1], core_recv.at[l, 1], sibling)

    def stage_d(l):
        sc[l].wait_recv()
        for h in range(2):
            s_t[l, :, half * h:half * h + half] = s_full[l, h].T
        other = s_t[l, pl.ds(pl.multiple_of(R * (1 - core), R), R), :]
        w = jnp.dot(other, merged[l, 1 - core], preferred_element_type=F32)
        for j in range(4):
            w_send[l, j] = w[:, 256 * j:256 * j + 256].astype(BF16)
        wc[l] = remote(w_send.at[l], w_recv.at[l], core_send.at[l, 2], core_recv.at[l, 2], sibling)
        mine = s_t[l, pl.ds(pl.multiple_of(R * core, R), R), :]
        w = jnp.dot(mine, merged[l, core], preferred_element_type=F32)
        for j in range(4):
            w_own[l, j] = w[:, 256 * j:256 * j + 256]

    def spread(l, phase, axis, source, target):
        return [
            remote(source((coord[axis] + k) % 4), target(k), ax_send.at[l, phase, k - 1], ax_recv.at[l, phase, k - 1], along(axis, k))
            for k in (1, 2, 3)
        ]

    ac = {}

    def axes(l):
        return l % 3, (l + 1) % 3, (l + 2) % 3

    def stage_e(l):
        wc[l].wait_recv()
        w_sum[l] = (w_own[l] + w_recv[l].astype(F32)).astype(BF16)
        ac[l, 0] = spread(l, 0, axes(l)[0], lambda j: w_sum.at[l, j], lambda k: r1.at[l, k - 1])

    def stage_f(l):
        for c in ac[l, 0]:
            c.wait_recv()
        total = w_sum[l, coord[axes(l)[0]]].astype(F32)
        for k in range(3):
            total = total + r1[l, k].astype(F32)
        mine = coord[axes(l)[1]]
        e1[l, mine] = total.astype(BF16)
        ac[l, 1] = spread(l, 1, axes(l)[1], lambda j: e1.at[l, mine], lambda k: e1.at[l, mine])

    def in_order(slots):
        return ((slots[0].astype(F32) + slots[1].astype(F32)) + slots[2].astype(F32)) + slots[3].astype(F32)

    def stage_h(l):
        for c in ac[l, 1]:
            c.wait_recv()
        mine = coord[axes(l)[2]]
        e2[l, mine] = in_order(e1.at[l]).astype(BF16)
        ac[l, 2] = spread(l, 2, axes(l)[2], lambda j: e2.at[l, mine], lambda k: e2.at[l, mine])

    def forward(l, j, k):
        piece = w_all.at[l, core, j]
        ac[l, 4, k] = remote(piece, piece, core_send.at[l, 4 + k], core_recv.at[l, 4 + k], sibling)

    def stage_i(l):
        for c in ac[l, 2]:
            c.wait_recv()
        mine = coord[axes(l)[0]]
        w_all[l, core, mine] = in_order(e2.at[l]).astype(BF16)
        piece = w_all.at[l, core, mine]
        ac[l, 3] = spread(l, 3, axes(l)[0], lambda j: piece, lambda k: piece)
        forward(l, mine, 0)

    def stage_k(l, k):
        ac[l, 3][k - 1].wait_recv()
        forward(l, (coord[axes(l)[0]] + 4 - k) % 4, k)

    gc = {}

    def gram_a():
        grams = []
        for l in range(LAYERS):
            mine = s_t[l, pl.ds(pl.multiple_of(R * core, R), R), :]
            grams.append(lax.dot_general(mine, mine, NT, preferred_element_type=F32))
        slot = coord[1]
        gram_y[slot, 0:64, :] = jnp.concatenate([grams[0], grams[1]], axis=1)
        gram_y[slot, 64:96, :] = jnp.concatenate([grams[2][0:32], grams[2][32:64]], axis=1)
        gc[0] = [
            remote(gram_y.at[slot], gram_y.at[slot], gram_send.at[0, k - 1], gram_recv.at[0, k - 1], along(1, k)) for k in (1, 2, 3)
        ]

    def gram_b():
        for c in gc[0]:
            c.wait_recv()
        slot = coord[2]
        gram_z[slot] = ((gram_y[0] + gram_y[1]) + gram_y[2]) + gram_y[3]
        gc[1] = [
            remote(gram_z.at[slot], gram_z.at[slot], gram_send.at[1, k - 1], gram_recv.at[1, k - 1], along(2, k)) for k in (1, 2, 3)
        ]

    def gram_c():
        for c in gc[1]:
            c.wait_recv()
        total = ((gram_z[0] + gram_z[1]) + gram_z[2]) + gram_z[3]
        lane = lax.broadcasted_iota(jnp.int32, (R, 2 * R), 1)
        row = lax.broadcasted_iota(jnp.int32, (R, 2 * R), 0)
        eye = (lane == row + R).astype(F32)
        both, last = total[0:64], total[64:96]
        aug[0] = jnp.where(lane < R, both, eye)
        aug[1] = jnp.where(lane < R, pltpu.roll(both, R, 1), eye)
        aug[2] = jnp.where(lane < R, jnp.concatenate([last, pltpu.roll(last, R, 1)], axis=0), eye)

    def eliminate(first, end):
        row = lax.broadcasted_iota(jnp.int32, (R, 2 * R), 0)

        def step(b, carry):
            left = row < R - 8 * b
            state = list(carry)
            for i in range(8):
                below = left & (row > i)
                for l in range(LAYERS):
                    a = state[l]
                    scaled = a[i:i + 1, :] / a[i:i + 1, i:i + 1]
                    state[l] = a - jnp.where(below, a[:, i:i + 1], 0.0) * scaled
            return tuple(pltpu.roll(jnp.concatenate([a[8:], a[:8]], axis=0), 2 * R - 8, 1) for a in state)

        done = lax.fori_loop(first, end, step, tuple(aug[l] for l in range(LAYERS)))
        for l in range(LAYERS):
            aug[l] = done[l]

    def invert():
        lane = lax.broadcasted_iota(jnp.int32, (R, 2 * R), 1)
        row = lax.broadcasted_iota(jnp.int32, (R, 2 * R), 0)
        for l in range(LAYERS):
            a = aug[l]
            pivots = jnp.sum(jnp.where(lane == row + R, a, 0.0), axis=1, keepdims=True)
            linv[l, core] = jnp.where(lane < R, a * lax.rsqrt(pivots), 0.0)
        gc[2] = [
            remote(linv.at[l, core], linv.at[l, core], core_send.at[l, 3], core_recv.at[l, 3], sibling) for l in range(LAYERS)
        ]

    def gram_d():
        for l in range(LAYERS):
            gc[2][l].wait_recv()
        for l in range(LAYERS):
            block = jnp.concatenate([linv[l, 0], pltpu.roll(linv[l, 1], R, 1)], axis=0)
            high = block.astype(BF16)
            low = (block - high.astype(F32)).astype(BF16)
            for h in range(2):
                s = s_full[l, h]
                out = lax.dot_general(s, high, NT, preferred_element_type=F32)
                out = out + lax.dot_general(s, low, NT, preferred_element_type=F32)
                basis[l, half * h:half * h + half, :] = out.astype(BF16)

    plan = [
        (stage_a, 0), (stage_a, 1), (stage_b, 0), (stage_a, 2), (stage_b, 1), (stage_b, 2),
        (stage_c, 0), (stage_c, 1), (stage_d, 0), (stage_c, 2), (stage_d, 1), (stage_e, 0), (stage_d, 2), (stage_e, 1), (stage_e, 2),
        (gram_a,), (stage_f, 0), (stage_f, 1), (stage_f, 2), (gram_b,), (stage_h, 0), (stage_h, 1), (stage_h, 2),
        (gram_c,), (eliminate, 0, 4), (stage_i, 0), (stage_i, 1), (stage_i, 2), (eliminate, 4, 8), (invert,),
        (stage_k, 0, 1), (stage_k, 1, 1), (stage_k, 2, 1), (stage_k, 0, 3), (stage_k, 1, 3), (stage_k, 2, 3),
        (stage_k, 0, 2), (stage_k, 1, 2), (stage_k, 2, 2), (gram_d,),
    ]
    for stage in plan:
        stage[0](*stage[1:])
    for l in range(LAYERS):
        for k in range(4):
            ac[l, 4, k].wait_recv()
    for c in sends:
        c.wait_send()


def rebuild_kernel(
    replicas, merged, basis, w_all, linv, memory_out, rebuilt_out, query_out, qpad, memory_buf, rebuilt_buf, query_buf, sem, query_sem
):
    copies = []

    def write(src, dst, s):
        c = pltpu.make_async_copy(src, dst, s)
        c.start()
        copies.append(c)

    for l in range(LAYERS):
        for m in range(2):
            inverse = linv[l, m][:, 0:R]
            high = inverse.astype(BF16)
            low = (inverse - high.astype(F32)).astype(BF16)
            qpad[l, m, R - R * m:2 * R - R * m, :] = jnp.zeros((R, KVW), BF16)
            for j in range(4):
                w = w_all[l, m, j]
                q = jnp.dot(high, w, preferred_element_type=F32) + jnp.dot(low, w, preferred_element_type=F32)
                q = q * (1.0 / replicas)
                query_buf[l, m, :, 256 * j:256 * j + 256] = q
                qpad[l, m, R * m:R * m + R, 256 * j:256 * j + 256] = q.astype(BF16)
            write(query_buf.at[l, m], query_out.at[l, m], query_sem.at[l, m])
            for n, r in enumerate(range(0, ROWS, CHUNK)):
                rows = slice(r, r + CHUNK)
                at = pl.ds(r, CHUNK)
                rebuilt = jnp.dot(basis[l, rows], qpad[l, m], preferred_element_type=F32)
                rebuilt_buf[l, m, rows] = rebuilt.astype(BF16)
                memory_buf[l, m, rows] = (merged[l, m, rows].astype(F32) - rebuilt).astype(BF16)
                write(rebuilt_buf.at[l, m, at], rebuilt_out.at[l, m, at], sem.at[l, m, n, 0])
                write(memory_buf.at[l, m, at], memory_out.at[0, l, m, at], sem.at[l, m, n, 1])
    for c in copies:
        c.wait()


def body(gradients, memory, initial_query):
    replicas = lax.axis_size("dp")
    vmem = pl.BlockSpec(memory_space=pltpu.VMEM)
    hbm = pl.BlockSpec(memory_space=pltpu.HBM)
    query_t = jnp.swapaxes(initial_query, 2, 3)
    half = ROWS // 2
    dma = pltpu.SemaphoreType.DMA
    merged, basis, w_all, linv = pl.pallas_call(
        reduce_kernel,
        name="reduce",
        out_shape=[
            pltpu.VMEM((LAYERS, 2, ROWS, KVW), BF16),
            pltpu.VMEM((LAYERS, ROWS, 2 * R), BF16),
            pltpu.VMEM((LAYERS, 2, 4, R, 256), BF16),
            pltpu.VMEM((LAYERS, 2, R, 2 * R), F32),
        ],
        in_specs=[hbm, hbm, hbm],
        out_specs=[vmem] * 4,
        scratch_shapes=[
            pltpu.VMEM((LAYERS, 2, ROWS, KVW), BF16),
            pltpu.VMEM((LAYERS, 2, ROWS, KVW), BF16),
            pltpu.VMEM((LAYERS, 2, R, KVW), F32),
            pltpu.VMEM((LAYERS, 2, KVW, 2 * R), BF16),
            pltpu.VMEM((LAYERS, ROWS, 2 * R), F32),
            pltpu.VMEM((LAYERS, half, 2 * R), BF16),
            pltpu.VMEM((LAYERS, half, 2 * R), BF16),
            pltpu.VMEM((LAYERS, 4, half, 2 * R), BF16),
            pltpu.VMEM((LAYERS, 2, half, 2 * R), BF16),
            pltpu.VMEM((LAYERS, 2 * R, ROWS), BF16),
            pltpu.VMEM((LAYERS, 4, R, 256), F32),
            pltpu.VMEM((LAYERS, 4, R, 256), BF16),
            pltpu.VMEM((LAYERS, 4, R, 256), BF16),
            pltpu.VMEM((LAYERS, 4, R, 256), BF16),
            pltpu.VMEM((LAYERS, 3, R, 256), BF16),
            pltpu.VMEM((LAYERS, 4, R, 256), BF16),
            pltpu.VMEM((LAYERS, 4, R, 256), BF16),
            pltpu.VMEM((4, 96, 2 * R), F32),
            pltpu.VMEM((4, 96, 2 * R), F32),
            pltpu.VMEM((LAYERS, R, 2 * R), F32),
            dma((LAYERS, 2, 2)),
            dma((LAYERS,)),
            dma((LAYERS, 8)),
            dma((LAYERS, 8)),
            dma((LAYERS, 3)),
            dma((LAYERS, 3)),
            dma((LAYERS, 4, 3)),
            dma((LAYERS, 4, 3)),
            dma((2, 3)),
            dma((2, 3)),
        ],
        compiler_params=pltpu.CompilerParams(collective_id=0, has_side_effects=True, vmem_limit_bytes=54 << 20),
    )(gradients, memory, query_t)

    new_memory, rebuilt, query = pl.pallas_call(
        functools.partial(rebuild_kernel, replicas),
        name="rebuild",
        out_shape=[
            jax.ShapeDtypeStruct((1, LAYERS, 2, ROWS, KVW), BF16),
            jax.ShapeDtypeStruct((LAYERS, 2, ROWS, KVW), BF16),
            jax.ShapeDtypeStruct((LAYERS, 2, R, KVW), F32),
        ],
        in_specs=[vmem] * 4,
        out_specs=[hbm] * 3,
        scratch_shapes=[
            pltpu.VMEM((LAYERS, 2, 2 * R, KVW), BF16),
            pltpu.VMEM((LAYERS, 2, ROWS, KVW), BF16),
            pltpu.VMEM((LAYERS, 2, ROWS, KVW), BF16),
            pltpu.VMEM((LAYERS, 2, R, KVW), F32),
            dma((LAYERS, 2, ROWS // CHUNK, 2)),
            dma((LAYERS, 2)),
        ],
        compiler_params=pltpu.CompilerParams(vmem_limit_bytes=36 << 20),
    )(merged, basis, w_all, linv)
    return new_memory, rebuilt, jnp.swapaxes(query, 2, 3)


def solution(mesh):
    in_specs = (P("dp", None, None, "tensor", None), P("dp", None, None, "tensor", None), P())
    out_specs = (P("dp", None, None, "tensor", None), P(None, None, "tensor", None), P())
    return jax.shard_map(body, mesh=mesh, in_specs=in_specs, out_specs=out_specs, check_vma=False)
```

```python
import functools

import jax
import jax.numpy as jnp
from jax import lax
from jax.experimental import pallas as pl
from jax.experimental.pallas import tpu as pltpu
from jax.sharding import PartitionSpec as P

MESH = pl.DeviceIdType.MESH
F32 = jnp.float32
BF16 = jnp.bfloat16
LAYERS = 3
ROWS = 512
KVW = 1024
R = 64
CHUNK = 256
DEPTH = 3
NT = (((1,), (1,)), ((), ()))


def reduce_kernel(
    g_hbm, m_hbm, query_hbm,
    merged, basis, w_all, linv,
    g_buf, m_buf, query, qpad, p_own, p_send, p_recv, x_own, x_part, s_full, s_t,
    w_own, w_send, w_recv, w_sum, r1, e1, e2, gram_y, gram_z, aug,
    load_sem, query_sem, core_send, core_recv, x_send, x_recv, ax_send, ax_recv, gram_send, gram_recv,
):
    dp = lax.axis_index("dp")
    tensor = lax.axis_index("tensor")
    core = dp % 2
    coord = (dp // 2, tensor // 4, tensor % 4)

    def along(axis, k):
        c = [coord[0], coord[1], coord[2]]
        c[axis] = (c[axis] + k) % 4
        return (c[0] * 2 + core, c[1] * 4 + c[2])

    sibling = (dp + 1 - 2 * core, tensor)

    query_loads = [pltpu.make_async_copy(query_hbm.at[l], query.at[l], query_sem.at[l]) for l in range(LAYERS)]
    loads = [
        (
            pltpu.make_async_copy(g_hbm.at[0, l, m], g_buf.at[l, m], load_sem.at[l, m, 0]),
            pltpu.make_async_copy(m_hbm.at[0, l, m], m_buf.at[l, m], load_sem.at[l, m, 1]),
        )
        for l in range(LAYERS)
        for m in range(2)
    ]

    def load(i):
        if i % 2 == 0:
            query_loads[i // 2].start()
        loads[i][0].start()
        loads[i][1].start()

    for i in range(DEPTH):
        load(i)

    barrier = pltpu.get_barrier_semaphore()
    pl.semaphore_signal(barrier, inc=1, device_id=sibling, device_id_type=MESH)
    for axis in range(3):
        for k in (1, 2, 3):
            pl.semaphore_signal(barrier, inc=1, device_id=along(axis, k), device_id_type=MESH)

    column = lax.broadcasted_iota(jnp.int32, (KVW, 2 * R), 1)

    def right_factor(l):
        query_loads[l].wait()
        pair = jnp.concatenate([query[l, 0], query[l, 1]], axis=0).astype(BF16).T
        for m in range(2):
            qpad[l, m] = jnp.where((column >= R * m) & (column < R * m + R), pair, jnp.zeros_like(pair))

    sends = []

    def remote(src, dst, send_sem, recv_sem, device):
        c = pltpu.make_async_remote_copy(src, dst, send_sem, recv_sem, device_id=device, device_id_type=MESH)
        c.start()
        sends.append(c)
        return c

    half = ROWS // 2
    pc, xc, sc, wc = {}, {}, {}, {}

    def stage_a(l):
        right_factor(l)
        for m in range(2):
            i = 2 * l + m
            loads[i][0].wait()
            loads[i][1].wait()
            if i + DEPTH < len(loads):
                load(i + DEPTH)
            for r in range(0, ROWS, CHUNK):
                rows = slice(r, r + CHUNK)
                block = g_buf[l, m, rows] + m_buf[l, m, rows]
                merged[l, m, rows] = block
                part = jnp.dot(block, qpad[l, m], preferred_element_type=F32)
                p_own[l, rows] = part if m == 0 else p_own[l, rows] + part
        p_send[l] = p_own[l, pl.ds(pl.multiple_of(half * (1 - core), half), half), :].astype(BF16)
        if l == 0:
            pl.semaphore_wait(barrier, 10)
        pc[l] = remote(p_send.at[l], p_recv.at[l], core_send.at[l, 0], core_recv.at[l, 0], sibling)

    def row64(j):
        return pl.ds(pl.multiple_of(j * 64, 64), 64)

    def stage_b(l):
        pc[l].wait_recv()
        mine = p_own[l, pl.ds(pl.multiple_of(half * core, half), half), :] + p_recv[l].astype(F32)
        x = coord[0]
        x_own[l] = mine.astype(BF16)
        xc[l] = [
            remote(x_own.at[l, row64((x + k) % 4)], x_part.at[l, k - 1], x_send.at[l, 0, k - 1], x_recv.at[l, 0, k - 1], along(0, k))
            for k in (1, 2, 3)
        ]

    def stage_r(l):
        for c in xc[l]:
            c.wait_recv()
        x = coord[0]
        total = x_own[l, row64(x), :].astype(F32)
        for k in range(3):
            total = total + x_part[l, k].astype(F32)
        piece = s_full.at[l, core, row64(x)]
        s_full[l, core, row64(x), :] = total.astype(BF16)
        xc[l] = [remote(piece, piece, x_send.at[l, 1, k - 1], x_recv.at[l, 1, k - 1], along(0, k)) for k in (1, 2, 3)]

    def stage_c(l):
        for c in xc[l]:
            c.wait_recv()
        sc[l] = remote(s_full.at[l, core], s_full.at[l, core], core_send.at[l, 1], core_recv.at[l, 1], sibling)

    def stage_d(l):
        sc[l].wait_recv()
        for h in range(2):
            s_t[l, :, half * h:half * h + half] = s_full[l, h].T
        other = s_t[l, pl.ds(pl.multiple_of(R * (1 - core), R), R), :]
        w = jnp.dot(other, merged[l, 1 - core], preferred_element_type=F32)
        for j in range(4):
            w_send[l, j] = w[:, 256 * j:256 * j + 256].astype(BF16)
        wc[l] = remote(w_send.at[l], w_recv.at[l], core_send.at[l, 2], core_recv.at[l, 2], sibling)
        mine = s_t[l, pl.ds(pl.multiple_of(R * core, R), R), :]
        w = jnp.dot(mine, merged[l, core], preferred_element_type=F32)
        for j in range(4):
            w_own[l, j] = w[:, 256 * j:256 * j + 256]

    def spread(l, phase, axis, source, target):
        return [
            remote(source((coord[axis] + k) % 4), target(k), ax_send.at[l, phase, k - 1], ax_recv.at[l, phase, k - 1], along(axis, k))
            for k in (1, 2, 3)
        ]

    ac = {}

    def axes(l):
        return l % 3, (l + 1) % 3, (l + 2) % 3

    def stage_e(l):
        wc[l].wait_recv()
        w_sum[l] = (w_own[l] + w_recv[l].astype(F32)).astype(BF16)
        ac[l, 0] = spread(l, 0, axes(l)[0], lambda j: w_sum.at[l, j], lambda k: r1.at[l, k - 1])

    def stage_f(l):
        for c in ac[l, 0]:
            c.wait_recv()
        total = w_sum[l, coord[axes(l)[0]]].astype(F32)
        for k in range(3):
            total = total + r1[l, k].astype(F32)
        mine = coord[axes(l)[1]]
        e1[l, mine] = total.astype(BF16)
        ac[l, 1] = spread(l, 1, axes(l)[1], lambda j: e1.at[l, mine], lambda k: e1.at[l, mine])

    def in_order(slots):
        return ((slots[0].astype(F32) + slots[1].astype(F32)) + slots[2].astype(F32)) + slots[3].astype(F32)

    def stage_h(l):
        for c in ac[l, 1]:
            c.wait_recv()
        mine = coord[axes(l)[2]]
        e2[l, mine] = in_order(e1.at[l]).astype(BF16)
        ac[l, 2] = spread(l, 2, axes(l)[2], lambda j: e2.at[l, mine], lambda k: e2.at[l, mine])

    def forward(l, j, k):
        piece = w_all.at[l, core, j]
        ac[l, 4, k] = remote(piece, piece, core_send.at[l, 4 + k], core_recv.at[l, 4 + k], sibling)

    def stage_i(l):
        for c in ac[l, 2]:
            c.wait_recv()
        mine = coord[axes(l)[0]]
        w_all[l, core, mine] = in_order(e2.at[l]).astype(BF16)
        piece = w_all.at[l, core, mine]
        ac[l, 3] = spread(l, 3, axes(l)[0], lambda j: piece, lambda k: piece)
        forward(l, mine, 0)

    def stage_k(l, k):
        ac[l, 3][k - 1].wait_recv()
        forward(l, (coord[axes(l)[0]] + 4 - k) % 4, k)

    gc = {}

    def gram_a():
        grams = []
        for l in range(LAYERS):
            mine = s_t[l, pl.ds(pl.multiple_of(R * core, R), R), :]
            grams.append(lax.dot_general(mine, mine, NT, preferred_element_type=F32))
        slot = coord[1]
        gram_y[slot, 0:64, :] = jnp.concatenate([grams[0], grams[1]], axis=1)
        gram_y[slot, 64:96, :] = jnp.concatenate([grams[2][0:32], grams[2][32:64]], axis=1)
        gc[0] = [
            remote(gram_y.at[slot], gram_y.at[slot], gram_send.at[0, k - 1], gram_recv.at[0, k - 1], along(1, k)) for k in (1, 2, 3)
        ]

    def gram_b():
        for c in gc[0]:
            c.wait_recv()
        slot = coord[2]
        gram_z[slot] = ((gram_y[0] + gram_y[1]) + gram_y[2]) + gram_y[3]
        gc[1] = [
            remote(gram_z.at[slot], gram_z.at[slot], gram_send.at[1, k - 1], gram_recv.at[1, k - 1], along(2, k)) for k in (1, 2, 3)
        ]

    def gram_c():
        for c in gc[1]:
            c.wait_recv()
        total = ((gram_z[0] + gram_z[1]) + gram_z[2]) + gram_z[3]
        lane = lax.broadcasted_iota(jnp.int32, (R, 2 * R), 1)
        row = lax.broadcasted_iota(jnp.int32, (R, 2 * R), 0)
        eye = (lane == row + R).astype(F32)
        both, last = total[0:64], total[64:96]
        aug[0] = jnp.where(lane < R, both, eye)
        aug[1] = jnp.where(lane < R, pltpu.roll(both, R, 1), eye)
        aug[2] = jnp.where(lane < R, jnp.concatenate([last, pltpu.roll(last, R, 1)], axis=0), eye)

    def eliminate(first, end):
        row = lax.broadcasted_iota(jnp.int32, (R, 2 * R), 0)

        def step(b, carry):
            left = row < R - 8 * b
            state = list(carry)
            for i in range(8):
                below = left & (row > i)
                for l in range(LAYERS):
                    a = state[l]
                    scaled = a[i:i + 1, :] / a[i:i + 1, i:i + 1]
                    state[l] = a - jnp.where(below, a[:, i:i + 1], 0.0) * scaled
            return tuple(pltpu.roll(jnp.concatenate([a[8:], a[:8]], axis=0), 2 * R - 8, 1) for a in state)

        done = lax.fori_loop(first, end, step, tuple(aug[l] for l in range(LAYERS)))
        for l in range(LAYERS):
            aug[l] = done[l]

    def invert():
        lane = lax.broadcasted_iota(jnp.int32, (R, 2 * R), 1)
        row = lax.broadcasted_iota(jnp.int32, (R, 2 * R), 0)
        for l in range(LAYERS):
            a = aug[l]
            pivots = jnp.sum(jnp.where(lane == row + R, a, 0.0), axis=1, keepdims=True)
            linv[l, core] = jnp.where(lane < R, a * lax.rsqrt(pivots), 0.0)
        gc[2] = [
            remote(linv.at[l, core], linv.at[l, core], core_send.at[l, 3], core_recv.at[l, 3], sibling) for l in range(LAYERS)
        ]

    def gram_d():
        for l in range(LAYERS):
            gc[2][l].wait_recv()
        for l in range(LAYERS):
            block = jnp.concatenate([linv[l, 0], pltpu.roll(linv[l, 1], R, 1)], axis=0)
            high = block.astype(BF16)
            low = (block - high.astype(F32)).astype(BF16)
            for h in range(2):
                s = s_full[l, h]
                out = lax.dot_general(s, high, NT, preferred_element_type=F32)
                out = out + lax.dot_general(s, low, NT, preferred_element_type=F32)
                basis[l, half * h:half * h + half, :] = out.astype(BF16)

    plan = [
        (stage_a, 0), (stage_a, 1), (stage_b, 0), (stage_a, 2), (stage_b, 1), (stage_b, 2),
        (stage_r, 0), (stage_r, 1), (stage_r, 2),
        (stage_c, 0), (stage_c, 1), (stage_d, 0), (stage_c, 2), (stage_d, 1), (stage_e, 0), (stage_d, 2), (stage_e, 1), (stage_e, 2),
        (gram_a,), (stage_f, 0), (stage_f, 1), (stage_f, 2), (gram_b,), (stage_h, 0), (stage_h, 1), (stage_h, 2),
        (gram_c,), (eliminate, 0, 4), (stage_i, 0), (stage_i, 1), (stage_i, 2), (eliminate, 4, 8), (invert,),
        (stage_k, 0, 1), (stage_k, 1, 1), (stage_k, 2, 1), (stage_k, 0, 3), (stage_k, 1, 3), (stage_k, 2, 3),
        (stage_k, 0, 2), (stage_k, 1, 2), (stage_k, 2, 2), (gram_d,),
    ]
    for stage in plan:
        stage[0](*stage[1:])
    for l in range(LAYERS):
        for k in range(4):
            ac[l, 4, k].wait_recv()
    for c in sends:
        c.wait_send()


def rebuild_kernel(
    replicas, merged, basis, w_all, linv, memory_out, rebuilt_out, query_out, qpad, memory_buf, rebuilt_buf, query_buf, sem, query_sem
):
    copies = []

    def write(src, dst, s):
        c = pltpu.make_async_copy(src, dst, s)
        c.start()
        copies.append(c)

    for l in range(LAYERS):
        for m in range(2):
            inverse = linv[l, m][:, 0:R]
            high = inverse.astype(BF16)
            low = (inverse - high.astype(F32)).astype(BF16)
            qpad[l, m, R - R * m:2 * R - R * m, :] = jnp.zeros((R, KVW), BF16)
            for j in range(4):
                w = w_all[l, m, j]
                q = jnp.dot(high, w, preferred_element_type=F32) + jnp.dot(low, w, preferred_element_type=F32)
                q = q * (1.0 / replicas)
                query_buf[l, m, :, 256 * j:256 * j + 256] = q
                qpad[l, m, R * m:R * m + R, 256 * j:256 * j + 256] = q.astype(BF16)
            write(query_buf.at[l, m], query_out.at[l, m], query_sem.at[l, m])
            for n, r in enumerate(range(0, ROWS, CHUNK)):
                rows = slice(r, r + CHUNK)
                at = pl.ds(r, CHUNK)
                rebuilt = jnp.dot(basis[l, rows], qpad[l, m], preferred_element_type=F32)
                rebuilt_buf[l, m, rows] = rebuilt.astype(BF16)
                memory_buf[l, m, rows] = (merged[l, m, rows].astype(F32) - rebuilt).astype(BF16)
                write(rebuilt_buf.at[l, m, at], rebuilt_out.at[l, m, at], sem.at[l, m, n, 0])
                write(memory_buf.at[l, m, at], memory_out.at[0, l, m, at], sem.at[l, m, n, 1])
    for c in copies:
        c.wait()


def body(gradients, memory, initial_query):
    replicas = lax.axis_size("dp")
    vmem = pl.BlockSpec(memory_space=pltpu.VMEM)
    hbm = pl.BlockSpec(memory_space=pltpu.HBM)
    query_t = jnp.swapaxes(initial_query, 2, 3)
    half = ROWS // 2
    dma = pltpu.SemaphoreType.DMA
    merged, basis, w_all, linv = pl.pallas_call(
        reduce_kernel,
        name="reduce",
        out_shape=[
            pltpu.VMEM((LAYERS, 2, ROWS, KVW), BF16),
            pltpu.VMEM((LAYERS, ROWS, 2 * R), BF16),
            pltpu.VMEM((LAYERS, 2, 4, R, 256), BF16),
            pltpu.VMEM((LAYERS, 2, R, 2 * R), F32),
        ],
        in_specs=[hbm, hbm, hbm],
        out_specs=[vmem] * 4,
        scratch_shapes=[
            pltpu.VMEM((LAYERS, 2, ROWS, KVW), BF16),
            pltpu.VMEM((LAYERS, 2, ROWS, KVW), BF16),
            pltpu.VMEM((LAYERS, 2, R, KVW), F32),
            pltpu.VMEM((LAYERS, 2, KVW, 2 * R), BF16),
            pltpu.VMEM((LAYERS, ROWS, 2 * R), F32),
            pltpu.VMEM((LAYERS, half, 2 * R), BF16),
            pltpu.VMEM((LAYERS, half, 2 * R), BF16),
            pltpu.VMEM((LAYERS, half, 2 * R), BF16),
            pltpu.VMEM((LAYERS, 3, 64, 2 * R), BF16),
            pltpu.VMEM((LAYERS, 2, half, 2 * R), BF16),
            pltpu.VMEM((LAYERS, 2 * R, ROWS), BF16),
            pltpu.VMEM((LAYERS, 4, R, 256), F32),
            pltpu.VMEM((LAYERS, 4, R, 256), BF16),
            pltpu.VMEM((LAYERS, 4, R, 256), BF16),
            pltpu.VMEM((LAYERS, 4, R, 256), BF16),
            pltpu.VMEM((LAYERS, 3, R, 256), BF16),
            pltpu.VMEM((LAYERS, 4, R, 256), BF16),
            pltpu.VMEM((LAYERS, 4, R, 256), BF16),
            pltpu.VMEM((4, 96, 2 * R), F32),
            pltpu.VMEM((4, 96, 2 * R), F32),
            pltpu.VMEM((LAYERS, R, 2 * R), F32),
            dma((LAYERS, 2, 2)),
            dma((LAYERS,)),
            dma((LAYERS, 8)),
            dma((LAYERS, 8)),
            dma((LAYERS, 2, 3)),
            dma((LAYERS, 2, 3)),
            dma((LAYERS, 4, 3)),
            dma((LAYERS, 4, 3)),
            dma((2, 3)),
            dma((2, 3)),
        ],
        compiler_params=pltpu.CompilerParams(collective_id=0, has_side_effects=True, vmem_limit_bytes=54 << 20),
    )(gradients, memory, query_t)

    new_memory, rebuilt, query = pl.pallas_call(
        functools.partial(rebuild_kernel, replicas),
        name="rebuild",
        out_shape=[
            jax.ShapeDtypeStruct((1, LAYERS, 2, ROWS, KVW), BF16),
            jax.ShapeDtypeStruct((LAYERS, 2, ROWS, KVW), BF16),
            jax.ShapeDtypeStruct((LAYERS, 2, R, KVW), F32),
        ],
        in_specs=[vmem] * 4,
        out_specs=[hbm] * 3,
        scratch_shapes=[
            pltpu.VMEM((LAYERS, 2, 2 * R, KVW), BF16),
            pltpu.VMEM((LAYERS, 2, ROWS, KVW), BF16),
            pltpu.VMEM((LAYERS, 2, ROWS, KVW), BF16),
            pltpu.VMEM((LAYERS, 2, R, KVW), F32),
            dma((LAYERS, 2, ROWS // CHUNK, 2)),
            dma((LAYERS, 2)),
        ],
        compiler_params=pltpu.CompilerParams(vmem_limit_bytes=36 << 20),
    )(merged, basis, w_all, linv)
    return new_memory, rebuilt, jnp.swapaxes(query, 2, 3)


def solution(mesh):
    in_specs = (P("dp", None, None, "tensor", None), P("dp", None, None, "tensor", None), P())
    out_specs = (P("dp", None, None, "tensor", None), P(None, None, "tensor", None), P())
    return jax.shard_map(body, mesh=mesh, in_specs=in_specs, out_specs=out_specs, check_vma=False)
```

```python
import functools

import jax
import jax.numpy as jnp
from jax import lax
from jax.experimental import pallas as pl
from jax.experimental.pallas import tpu as pltpu
from jax.sharding import PartitionSpec as P

MESH = pl.DeviceIdType.MESH
F32 = jnp.float32
BF16 = jnp.bfloat16
LAYERS = 3
ROWS = 512
KVW = 1024
R = 64
CHUNK = 256
DEPTH = 4
NT = (((1,), (1,)), ((), ()))


def reduce_kernel(
    g_hbm, m_hbm, query_hbm,
    merged, basis, w_all, linv,
    g_buf, m_buf, query, qpad, p_own, p_send, p_recv, x_own, x_part, s_full, s_t,
    w_own, w_send, w_recv, w_sum, r1, e1, e2, gram_y, gram_z, aug,
    load_sem, query_sem, send, core_recv, x_recv, w_arrive, gram_recv, end_recv,
):
    dp = lax.axis_index("dp")
    tensor = lax.axis_index("tensor")
    core = dp % 2
    coord = (dp // 2, tensor // 4, tensor % 4)

    def along(axis, k):
        c = [coord[0], coord[1], coord[2]]
        c[axis] = (c[axis] + k) % 4
        return (c[0] * 2 + core, c[1] * 4 + c[2])

    sibling = (dp + 1 - 2 * core, tensor)

    query_loads = [pltpu.make_async_copy(query_hbm.at[l], query.at[l], query_sem.at[l]) for l in range(LAYERS)]
    loads = [
        (
            pltpu.make_async_copy(g_hbm.at[0, l, m], g_buf.at[l, m], load_sem.at[l, m]),
            pltpu.make_async_copy(m_hbm.at[0, l, m], m_buf.at[l, m], load_sem.at[l, m]),
        )
        for l in range(LAYERS)
        for m in range(2)
    ]

    def load(i):
        if i % 2 == 0:
            query_loads[i // 2].start()
        loads[i][0].start()
        loads[i][1].start()

    for i in range(DEPTH):
        load(i)

    barrier = pltpu.get_barrier_semaphore()
    pl.semaphore_signal(barrier, inc=1, device_id=sibling, device_id_type=MESH)
    for axis in range(3):
        for k in (1, 2, 3):
            pl.semaphore_signal(barrier, inc=1, device_id=along(axis, k), device_id_type=MESH)

    column = lax.broadcasted_iota(jnp.int32, (KVW, 2 * R), 1)

    def right_factor(l):
        query_loads[l].wait()
        pair = jnp.concatenate([query[l, 0], query[l, 1]], axis=0).astype(BF16).T
        for m in range(2):
            qpad[l, m] = jnp.where((column >= R * m) & (column < R * m + R), pair, jnp.zeros_like(pair))

    def remote(src, dst, send_sem, recv_sem, device):
        c = pltpu.make_async_remote_copy(src, dst, send_sem, recv_sem, device_id=device, device_id_type=MESH)
        c.start()
        return c

    def drain(like, sem):
        pltpu.make_async_copy(like, like, sem).wait()

    half = ROWS // 2

    def stage_a(l):
        right_factor(l)
        for m in range(2):
            i = 2 * l + m
            drain(g_buf.at[0], load_sem.at[l, m])
            if i + DEPTH < len(loads):
                load(i + DEPTH)
            for r in range(0, ROWS, CHUNK):
                rows = slice(r, r + CHUNK)
                block = g_buf[l, m, rows] + m_buf[l, m, rows]
                merged[l, m, rows] = block
                part = jnp.dot(block, qpad[l, m], preferred_element_type=F32)
                p_own[l, rows] = part if m == 0 else p_own[l, rows] + part
        p_send[l] = p_own[l, pl.ds(pl.multiple_of(half * (1 - core), half), half), :].astype(BF16)
        if l == 0:
            pl.semaphore_wait(barrier, 10)
        remote(p_send.at[l], p_recv.at[l], send.at[0], core_recv.at[l, 0], sibling)

    def row64(j):
        return pl.ds(pl.multiple_of(j * 64, 64), 64)

    def stage_b(l):
        drain(p_recv.at[l], core_recv.at[l, 0])
        mine = p_own[l, pl.ds(pl.multiple_of(half * core, half), half), :] + p_recv[l].astype(F32)
        x = coord[0]
        x_own[l] = mine.astype(BF16)
        for k in (1, 2, 3):
            remote(x_own.at[l, row64((x + k) % 4)], x_part.at[l, k - 1], send.at[1], x_recv.at[l, 0], along(0, k))

    def stage_r(l):
        drain(x_part.at[l], x_recv.at[l, 0])
        x = coord[0]
        total = x_own[l, row64(x), :].astype(F32)
        for k in range(3):
            total = total + x_part[l, k].astype(F32)
        piece = s_full.at[l, core, row64(x)]
        s_full[l, core, row64(x), :] = total.astype(BF16)
        for k in (1, 2, 3):
            remote(piece, piece, send.at[2], x_recv.at[l, 1], along(0, k))

    def stage_c(l):
        drain(x_part.at[l], x_recv.at[l, 1])
        remote(s_full.at[l, core], s_full.at[l, core], send.at[3], core_recv.at[l, 1], sibling)

    def stage_d(l):
        drain(p_recv.at[l], core_recv.at[l, 1])
        for h in range(2):
            s_t[l, :, half * h:half * h + half] = s_full[l, h].T
        other = s_t[l, pl.ds(pl.multiple_of(R * (1 - core), R), R), :]
        w = jnp.dot(other, merged[l, 1 - core], preferred_element_type=F32)
        for j in range(4):
            w_send[l, j] = w[:, 256 * j:256 * j + 256].astype(BF16)
        remote(w_send.at[l], w_recv.at[l], send.at[4], core_recv.at[l, 2], sibling)
        mine = s_t[l, pl.ds(pl.multiple_of(R * core, R), R), :]
        w = jnp.dot(mine, merged[l, core], preferred_element_type=F32)
        for j in range(4):
            w_own[l, j] = w[:, 256 * j:256 * j + 256]

    def axes(l, h):
        return (l + h) % 3, (l + h + 1) % 3, (l + h + 2) % 3

    def stage_e(l):
        drain(w_recv.at[l], core_recv.at[l, 2])
        w_sum[l] = (w_own[l] + w_recv[l].astype(F32)).astype(BF16)
        for h in range(2):
            axis = axes(l, h)[0]
            for k in (1, 2, 3):
                piece = w_sum.at[l, (coord[axis] + k) % 4, pl.ds(32 * h, 32)]
                remote(piece, r1.at[l, h, k - 1], send.at[5], w_arrive.at[l, h, 0], along(axis, k))

    def exchange(slots, l, h, phase, value):
        axis = axes(l, h)[phase]
        piece = slots.at[l, h, coord[axis]]
        slots[l, h, coord[axis]] = value.astype(BF16)
        for k in (1, 2, 3):
            remote(piece, piece, send.at[5 + phase], w_arrive.at[l, h, phase], along(axis, k))

    def stage_f(l):
        for h in range(2):
            drain(r1.at[l, h], w_arrive.at[l, h, 0])
            total = w_sum[l, coord[axes(l, h)[0]], 32 * h:32 * h + 32, :].astype(F32)
            for k in range(3):
                total = total + r1[l, h, k].astype(F32)
            exchange(e1, l, h, 1, total)

    def in_order(slots):
        return ((slots[0].astype(F32) + slots[1].astype(F32)) + slots[2].astype(F32)) + slots[3].astype(F32)

    def stage_h(l):
        for h in range(2):
            drain(r1.at[l, h], w_arrive.at[l, h, 1])
            exchange(e2, l, h, 2, in_order(e1.at[l, h]))

    def forward(l, h, j):
        piece = w_all.at[l, core, j, pl.ds(32 * h, 32)]
        remote(piece, piece, send.at[9], end_recv.at[0], sibling)

    def stage_i(l):
        for h in range(2):
            drain(r1.at[l, h], w_arrive.at[l, h, 2])
            axis = axes(l, h)[0]
            mine = coord[axis]
            w_all[l, core, mine, 32 * h:32 * h + 32, :] = in_order(e2.at[l, h]).astype(BF16)
            piece = w_all.at[l, core, mine, pl.ds(32 * h, 32)]
            for k in (1, 2, 3):
                remote(piece, piece, send.at[8], w_arrive.at[l, h, 2 + k], along(axis, k))
            forward(l, h, mine)

    def stage_k(l, k):
        for h in range(2):
            drain(r1.at[l, h, 0], w_arrive.at[l, h, 2 + k])
            forward(l, h, (coord[axes(l, h)[0]] + 4 - k) % 4)

    def gram(l):
        mine = s_t[l, pl.ds(pl.multiple_of(R * core, R), R), :]
        return lax.dot_general(mine, mine, NT, preferred_element_type=F32)

    def gram_a(first, rows):
        slot = coord[1]
        if first == 0:
            gram_y[slot, 0:64, :] = jnp.concatenate([gram(0), gram(1)], axis=1)
        else:
            last = gram(2)
            gram_y[slot, 64:96, :] = jnp.concatenate([last[0:32], last[32:64]], axis=1)
        piece = gram_y.at[slot, pl.ds(first, rows)]
        for k in (1, 2, 3):
            remote(piece, piece, send.at[10], gram_recv.at[first // 64], along(1, k))

    def gram_b():
        drain(gram_y.at[pl.ds(0, 3), pl.ds(0, 64)], gram_recv.at[0])
        drain(gram_y.at[pl.ds(0, 3), pl.ds(64, 32)], gram_recv.at[1])
        slot = coord[2]
        gram_z[slot] = ((gram_y[0] + gram_y[1]) + gram_y[2]) + gram_y[3]
        for k in (1, 2, 3):
            remote(gram_z.at[slot], gram_z.at[slot], send.at[11], gram_recv.at[2], along(2, k))

    def gram_c():
        drain(gram_z.at[pl.ds(0, 3)], gram_recv.at[2])
        total = ((gram_z[0] + gram_z[1]) + gram_z[2]) + gram_z[3]
        lane = lax.broadcasted_iota(jnp.int32, (R, 2 * R), 1)
        row = lax.broadcasted_iota(jnp.int32, (R, 2 * R), 0)
        eye = (lane == row + R).astype(F32)
        both, last = total[0:64], total[64:96]
        aug[0] = jnp.where(lane < R, both, eye)
        aug[1] = jnp.where(lane < R, pltpu.roll(both, R, 1), eye)
        aug[2] = jnp.where(lane < R, jnp.concatenate([last, pltpu.roll(last, R, 1)], axis=0), eye)

    def eliminate(first, end):
        row = lax.broadcasted_iota(jnp.int32, (R, 2 * R), 0)

        def step(b, carry):
            left = row < R - 8 * b
            state = list(carry)
            for i in range(8):
                below = left & (row > i)
                for l in range(LAYERS):
                    a = state[l]
                    scaled = a[i:i + 1, :] / a[i:i + 1, i:i + 1]
                    state[l] = a - jnp.where(below, a[:, i:i + 1], 0.0) * scaled
            return tuple(pltpu.roll(jnp.concatenate([a[8:], a[:8]], axis=0), 2 * R - 8, 1) for a in state)

        done = lax.fori_loop(first, end, step, tuple(aug[l] for l in range(LAYERS)))
        for l in range(LAYERS):
            aug[l] = done[l]

    def invert():
        lane = lax.broadcasted_iota(jnp.int32, (R, 2 * R), 1)
        row = lax.broadcasted_iota(jnp.int32, (R, 2 * R), 0)
        for l in range(LAYERS):
            a = aug[l]
            pivots = jnp.sum(jnp.where(lane == row + R, a, 0.0), axis=1, keepdims=True)
            linv[l, core] = jnp.where(lane < R, a * lax.rsqrt(pivots), 0.0)
            remote(linv.at[l, core], linv.at[l, core], send.at[12], end_recv.at[1], sibling)

    def gram_d():
        drain(aug, end_recv.at[1])
        for l in range(LAYERS):
            block = jnp.concatenate([linv[l, 0], pltpu.roll(linv[l, 1], R, 1)], axis=0)
            high = block.astype(BF16)
            low = (block - high.astype(F32)).astype(BF16)
            for h in range(2):
                s = s_full[l, h]
                out = lax.dot_general(s, high, NT, preferred_element_type=F32)
                out = out + lax.dot_general(s, low, NT, preferred_element_type=F32)
                basis[l, half * h:half * h + half, :] = out.astype(BF16)

    plan = [
        (stage_a, 0), (stage_a, 1), (stage_b, 0), (stage_a, 2), (stage_b, 1), (stage_b, 2),
        (stage_r, 0), (stage_r, 1), (stage_r, 2),
        (stage_c, 0), (stage_c, 1), (stage_d, 0), (stage_c, 2), (stage_d, 1), (stage_e, 0), (stage_d, 2), (stage_e, 1),
        (gram_a, 0, 64), (stage_e, 2), (gram_a, 64, 32),
        (stage_f, 0), (stage_f, 1), (stage_f, 2), (gram_b,), (stage_h, 0), (stage_h, 1), (stage_h, 2),
        (gram_c,), (eliminate, 0, 4), (stage_i, 0), (stage_i, 1), (stage_i, 2), (eliminate, 4, 8), (invert,),
        (stage_k, 0, 1), (stage_k, 0, 3), (stage_k, 0, 2), (stage_k, 1, 1), (stage_k, 1, 3), (stage_k, 1, 2),
        (stage_k, 2, 1), (stage_k, 2, 3), (stage_k, 2, 2), (gram_d,),
    ]
    for stage in plan:
        stage[0](*stage[1:])
    drain(w_recv, end_recv.at[0])
    for n, like in enumerate(
        (p_recv, x_part, x_part, p_recv, w_recv, r1, r1, r1, r1, w_recv, gram_y.at[pl.ds(0, 3)], gram_z.at[pl.ds(0, 3)], aug)
    ):
        drain(like, send.at[n])


def rebuild_kernel(
    replicas, merged, basis, w_all, linv, memory_out, rebuilt_out, query_out, qpad, memory_buf, rebuilt_buf, query_buf, sem
):
    def write(src, dst, n):
        pltpu.make_async_copy(src, dst, sem.at[n]).start()

    for l in range(LAYERS):
        for m in range(2):
            inverse = linv[l, m][:, 0:R]
            high = inverse.astype(BF16)
            low = (inverse - high.astype(F32)).astype(BF16)
            qpad[l, m, R - R * m:2 * R - R * m, :] = jnp.zeros((R, KVW), BF16)
            for j in range(4):
                w = w_all[l, m, j]
                q = jnp.dot(high, w, preferred_element_type=F32) + jnp.dot(low, w, preferred_element_type=F32)
                q = q * (1.0 / replicas)
                query_buf[l, m, :, 256 * j:256 * j + 256] = q
                qpad[l, m, R * m:R * m + R, 256 * j:256 * j + 256] = q.astype(BF16)
            write(query_buf.at[l, m], query_out.at[l, m], 0)
            for r in range(0, ROWS, CHUNK):
                rows = slice(r, r + CHUNK)
                at = pl.ds(r, CHUNK)
                rebuilt = jnp.dot(basis[l, rows], qpad[l, m], preferred_element_type=F32)
                rebuilt_buf[l, m, rows] = rebuilt.astype(BF16)
                memory_buf[l, m, rows] = (merged[l, m, rows].astype(F32) - rebuilt).astype(BF16)
                write(rebuilt_buf.at[l, m, at], rebuilt_out.at[l, m, at], 1)
                write(memory_buf.at[l, m, at], memory_out.at[0, l, m, at], 2)
    for n, buffer in enumerate((query_buf, rebuilt_buf, memory_buf)):
        pltpu.make_async_copy(buffer, buffer, sem.at[n]).wait()


def body(gradients, memory, initial_query):
    replicas = lax.axis_size("dp")
    vmem = pl.BlockSpec(memory_space=pltpu.VMEM)
    hbm = pl.BlockSpec(memory_space=pltpu.HBM)
    query_t = jnp.swapaxes(initial_query, 2, 3)
    half = ROWS // 2
    dma = pltpu.SemaphoreType.DMA
    merged, basis, w_all, linv = pl.pallas_call(
        reduce_kernel,
        name="reduce",
        out_shape=[
            pltpu.VMEM((LAYERS, 2, ROWS, KVW), BF16),
            pltpu.VMEM((LAYERS, ROWS, 2 * R), BF16),
            pltpu.VMEM((LAYERS, 2, 4, R, 256), BF16),
            pltpu.VMEM((LAYERS, 2, R, 2 * R), F32),
        ],
        in_specs=[hbm, hbm, hbm],
        out_specs=[vmem] * 4,
        scratch_shapes=[
            pltpu.VMEM((LAYERS, 2, ROWS, KVW), BF16),
            pltpu.VMEM((LAYERS, 2, ROWS, KVW), BF16),
            pltpu.VMEM((LAYERS, 2, R, KVW), F32),
            pltpu.VMEM((LAYERS, 2, KVW, 2 * R), BF16),
            pltpu.VMEM((LAYERS, ROWS, 2 * R), F32),
            pltpu.VMEM((LAYERS, half, 2 * R), BF16),
            pltpu.VMEM((LAYERS, half, 2 * R), BF16),
            pltpu.VMEM((LAYERS, half, 2 * R), BF16),
            pltpu.VMEM((LAYERS, 3, 64, 2 * R), BF16),
            pltpu.VMEM((LAYERS, 2, half, 2 * R), BF16),
            pltpu.VMEM((LAYERS, 2 * R, ROWS), BF16),
            pltpu.VMEM((LAYERS, 4, R, 256), F32),
            pltpu.VMEM((LAYERS, 4, R, 256), BF16),
            pltpu.VMEM((LAYERS, 4, R, 256), BF16),
            pltpu.VMEM((LAYERS, 4, R, 256), BF16),
            pltpu.VMEM((LAYERS, 2, 3, 32, 256), BF16),
            pltpu.VMEM((LAYERS, 2, 4, 32, 256), BF16),
            pltpu.VMEM((LAYERS, 2, 4, 32, 256), BF16),
            pltpu.VMEM((4, 96, 2 * R), F32),
            pltpu.VMEM((4, 96, 2 * R), F32),
            pltpu.VMEM((LAYERS, R, 2 * R), F32),
            dma((LAYERS, 2)),
            dma((LAYERS,)),
            dma((13,)),
            dma((LAYERS, 3)),
            dma((LAYERS, 2)),
            dma((LAYERS, 2, 6)),
            dma((3,)),
            dma((2,)),
        ],
        compiler_params=pltpu.CompilerParams(collective_id=0, has_side_effects=True, vmem_limit_bytes=54 << 20),
    )(gradients, memory, query_t)

    new_memory, rebuilt, query = pl.pallas_call(
        functools.partial(rebuild_kernel, replicas),
        name="rebuild",
        out_shape=[
            jax.ShapeDtypeStruct((1, LAYERS, 2, ROWS, KVW), BF16),
            jax.ShapeDtypeStruct((LAYERS, 2, ROWS, KVW), BF16),
            jax.ShapeDtypeStruct((LAYERS, 2, R, KVW), F32),
        ],
        in_specs=[vmem] * 4,
        out_specs=[hbm] * 3,
        scratch_shapes=[
            pltpu.VMEM((LAYERS, 2, 2 * R, KVW), BF16),
            pltpu.VMEM((LAYERS, 2, ROWS, KVW), BF16),
            pltpu.VMEM((LAYERS, 2, ROWS, KVW), BF16),
            pltpu.VMEM((LAYERS, 2, R, KVW), F32),
            dma((3,)),
        ],
        compiler_params=pltpu.CompilerParams(vmem_limit_bytes=36 << 20),
    )(merged, basis, w_all, linv)
    return new_memory, rebuilt, jnp.swapaxes(query, 2, 3)


def solution(mesh):
    in_specs = (P("dp", None, None, "tensor", None), P("dp", None, None, "tensor", None), P())
    out_specs = (P("dp", None, None, "tensor", None), P(None, None, "tensor", None), P())
    return jax.shard_map(body, mesh=mesh, in_specs=in_specs, out_specs=out_specs, check_vma=False)
```

```python
import functools

import jax
import jax.numpy as jnp
from jax import lax
from jax.experimental import pallas as pl
from jax.experimental.pallas import tpu as pltpu
from jax.sharding import PartitionSpec as P

MESH = pl.DeviceIdType.MESH
F32 = jnp.float32
BF16 = jnp.bfloat16
LAYERS = 3
ROWS = 512
KVW = 1024
R = 64
CHUNK = 256
DEPTH = 4
NT = (((1,), (1,)), ((), ()))


def reduce_kernel(
    g_hbm, m_hbm, query_hbm,
    merged, basis, w_all, linv,
    g_buf, m_buf, query, qpad, p_own, p_send, p_part, s_full, s_t, w_send, r1, e1, e2, gram_y, gram_z, aug,
    load_sem, query_sem, send, s_recv, w_arrive, gram_recv, linv_recv,
):
    dp = lax.axis_index("dp")
    tensor = lax.axis_index("tensor")
    core = dp % 2
    coord = (dp // 2, tensor // 4, tensor % 4)

    def along(axis, k, other=0):
        c = [coord[0], coord[1], coord[2]]
        c[axis] = (c[axis] + k) % 4
        return (c[0] * 2 + (core + other) % 2, c[1] * 4 + c[2])

    sibling = (dp + 1 - 2 * core, tensor)

    query_loads = [pltpu.make_async_copy(query_hbm.at[l], query.at[l], query_sem.at[l]) for l in range(LAYERS)]
    loads = [
        (
            pltpu.make_async_copy(g_hbm.at[0, l, m], g_buf.at[l, m], load_sem.at[l, m]),
            pltpu.make_async_copy(m_hbm.at[0, l, m], m_buf.at[l, m], load_sem.at[l, m]),
        )
        for l in range(LAYERS)
        for m in range(2)
    ]

    def load(i):
        if i % 2 == 0:
            query_loads[i // 2].start()
        loads[i][0].start()
        loads[i][1].start()

    for i in range(DEPTH):
        load(i)

    barrier = pltpu.get_barrier_semaphore()
    pl.semaphore_signal(barrier, inc=1, device_id=sibling, device_id_type=MESH)
    for axis in range(3):
        for k in (1, 2, 3):
            for other in range(2):
                pl.semaphore_signal(barrier, inc=1, device_id=along(axis, k, other), device_id_type=MESH)

    column = lax.broadcasted_iota(jnp.int32, (KVW, 2 * R), 1)

    def right_factor(l):
        query_loads[l].wait()
        pair = jnp.concatenate([query[l, 0], query[l, 1]], axis=0).astype(BF16).T
        for m in range(2):
            qpad[l, m] = jnp.where((column >= R * m) & (column < R * m + R), pair, jnp.zeros_like(pair))

    def remote(src, dst, send_sem, recv_sem, device):
        c = pltpu.make_async_remote_copy(src, dst, send_sem, recv_sem, device_id=device, device_id_type=MESH)
        c.start()
        return c

    def drain(like, sem):
        pltpu.make_async_copy(like, like, sem).wait()

    partners = [(k, other) for k in (2, 1, 3) for other in range(2)] + [(0, 1)]
    half = ROWS // 2

    def row64(j):
        return pl.ds(pl.multiple_of(j * 64, 64), 64)

    def stage_a(l):
        right_factor(l)
        for m in range(2):
            i = 2 * l + m
            drain(g_buf.at[0], load_sem.at[l, m])
            if i + DEPTH < len(loads):
                load(i + DEPTH)
            for r in range(0, ROWS, CHUNK):
                rows = slice(r, r + CHUNK)
                block = g_buf[l, m, rows] + m_buf[l, m, rows]
                merged[l, m, rows] = block
                part = jnp.dot(block, qpad[l, m], preferred_element_type=F32)
                p_own[l, rows] = part if m == 0 else p_own[l, rows] + part
        p_send[l] = p_own[l].astype(BF16)
        if l == 0:
            pl.semaphore_wait(barrier, 19)
        for n, (k, other) in enumerate(partners):
            owner = (coord[0] + k) % 4 * 2 + (core + other) % 2
            remote(p_send.at[l, row64(owner)], p_part.at[l, n], send.at[0], s_recv.at[l, 0], along(0, k, other))

    def stage_r(l):
        drain(p_part.at[l], s_recv.at[l, 0])
        total = p_send[l, row64(dp), :].astype(F32)
        for n in range(len(partners)):
            total = total + p_part[l, n].astype(F32)
        piece = s_full.at[l, row64(dp)]
        s_full[l, row64(dp), :] = total.astype(BF16)
        for k, other in partners:
            remote(piece, piece, send.at[1], s_recv.at[l, 1], along(0, k, other))

    def stage_d(l):
        drain(p_part.at[l], s_recv.at[l, 1])
        s_t[l] = s_full[l].T
        for m in range(2):
            w = jnp.dot(s_t[l, R * m:R * m + R, :], merged[l, m], preferred_element_type=F32)
            for j in range(4):
                w_send[l, m, j] = w[:, 256 * j:256 * j + 256].astype(BF16)
        for h in range(2):
            axis = axes(l, h)[0]
            for n, (k, other) in enumerate(partners):
                piece = w_send.at[l, (core + other) % 2, (coord[axis] + k) % 4, pl.ds(32 * h, 32)]
                remote(piece, r1.at[l, h, n], send.at[2], w_arrive.at[l, h, 0], along(axis, k, other))

    def axes(l, h):
        return (l + h) % 3, (l + h + 1) % 3, (l + h + 2) % 3

    def exchange(slots, l, h, phase, value):
        axis = axes(l, h)[phase]
        piece = slots.at[l, h, coord[axis]]
        slots[l, h, coord[axis]] = value.astype(BF16)
        for k in (1, 2, 3):
            remote(piece, piece, send.at[2 + phase], w_arrive.at[l, h, phase], along(axis, k))

    def stage_f(l):
        for h in range(2):
            drain(r1.at[l, h], w_arrive.at[l, h, 0])
            total = w_send[l, core, coord[axes(l, h)[0]], 32 * h:32 * h + 32, :].astype(F32)
            for n in range(len(partners)):
                total = total + r1[l, h, n].astype(F32)
            exchange(e1, l, h, 1, total)

    def in_order(slots):
        return ((slots[0].astype(F32) + slots[1].astype(F32)) + slots[2].astype(F32)) + slots[3].astype(F32)

    def stage_h(l):
        for h in range(2):
            drain(r1.at[l, h, pl.ds(0, 3)], w_arrive.at[l, h, 1])
            exchange(e2, l, h, 2, in_order(e1.at[l, h]))

    def stage_i(l):
        for h in range(2):
            drain(r1.at[l, h, pl.ds(0, 3)], w_arrive.at[l, h, 2])
            axis = axes(l, h)[0]
            mine = coord[axis]
            w_all[l, core, mine, 32 * h:32 * h + 32, :] = in_order(e2.at[l, h]).astype(BF16)
            piece = w_all.at[l, core, mine, pl.ds(32 * h, 32)]
            for k, other in partners:
                remote(piece, piece, send.at[5], w_arrive.at[l, h, 3], along(axis, k, other))

    def stage_k(l):
        for h in range(2):
            drain(r1.at[l, h], w_arrive.at[l, h, 3])

    def gram(l):
        mine = s_t[l, pl.ds(pl.multiple_of(R * core, R), R), :]
        return lax.dot_general(mine, mine, NT, preferred_element_type=F32)

    def gram_a(first, rows):
        slot = coord[1]
        if first == 0:
            gram_y[slot, 0:64, :] = jnp.concatenate([gram(0), gram(1)], axis=1)
        else:
            last = gram(2)
            gram_y[slot, 64:96, :] = jnp.concatenate([last[0:32], last[32:64]], axis=1)
        piece = gram_y.at[slot, pl.ds(first, rows)]
        for k in (1, 2, 3):
            remote(piece, piece, send.at[6], gram_recv.at[first // 64], along(1, k))

    def gram_b():
        drain(gram_y.at[pl.ds(0, 3), pl.ds(0, 64)], gram_recv.at[0])
        drain(gram_y.at[pl.ds(0, 3), pl.ds(64, 32)], gram_recv.at[1])
        slot = coord[2]
        gram_z[slot] = ((gram_y[0] + gram_y[1]) + gram_y[2]) + gram_y[3]
        for k in (1, 2, 3):
            remote(gram_z.at[slot], gram_z.at[slot], send.at[7], gram_recv.at[2], along(2, k))

    def gram_c():
        drain(gram_z.at[pl.ds(0, 3)], gram_recv.at[2])
        total = ((gram_z[0] + gram_z[1]) + gram_z[2]) + gram_z[3]
        lane = lax.broadcasted_iota(jnp.int32, (R, 2 * R), 1)
        row = lax.broadcasted_iota(jnp.int32, (R, 2 * R), 0)
        eye = (lane == row + R).astype(F32)
        both, last = total[0:64], total[64:96]
        aug[0] = jnp.where(lane < R, both, eye)
        aug[1] = jnp.where(lane < R, pltpu.roll(both, R, 1), eye)
        aug[2] = jnp.where(lane < R, jnp.concatenate([last, pltpu.roll(last, R, 1)], axis=0), eye)

    def eliminate(first, end):
        row = lax.broadcasted_iota(jnp.int32, (8, 2 * R), 0)
        state = [aug[l, 8 * first:R, :] for l in range(LAYERS)]
        for b in range(first, end):
            top = [a[0:8] for a in state]
            state = [a[8:] for a in state]
            for i in range(8):
                j = 8 * b + i
                for l in range(LAYERS):
                    scaled = top[l][i:i + 1, :] / top[l][i:i + 1, j:j + 1]
                    top[l] = top[l] - jnp.where(row > i, top[l][:, j:j + 1], 0.0) * scaled
                    if j < R - 8:
                        state[l] = state[l] - state[l][:, j:j + 1] * scaled
            for l in range(LAYERS):
                aug[l, 8 * b:8 * b + 8, :] = top[l]
        if end < R // 8:
            for l in range(LAYERS):
                aug[l, 8 * end:R, :] = state[l]

    def invert():
        lane = lax.broadcasted_iota(jnp.int32, (R, 2 * R), 1)
        row = lax.broadcasted_iota(jnp.int32, (R, 2 * R), 0)
        for l in range(LAYERS):
            a = aug[l]
            pivots = jnp.sum(jnp.where(lane == row, a, 0.0), axis=1, keepdims=True)
            linv[l, core] = jnp.where(lane < R, pltpu.roll(a, R, 1) * lax.rsqrt(pivots), 0.0)
            remote(linv.at[l, core], linv.at[l, core], send.at[8], linv_recv, sibling)

    def gram_d():
        drain(aug, linv_recv)
        for l in range(LAYERS):
            block = jnp.concatenate([linv[l, 0], pltpu.roll(linv[l, 1], R, 1)], axis=0)
            high = block.astype(BF16)
            low = (block - high.astype(F32)).astype(BF16)
            for h in range(2):
                s = s_full[l, half * h:half * h + half, :]
                out = lax.dot_general(s, high, NT, preferred_element_type=F32)
                out = out + lax.dot_general(s, low, NT, preferred_element_type=F32)
                basis[l, half * h:half * h + half, :] = out.astype(BF16)

    plan = [
        (stage_a, 0), (stage_a, 1), (stage_a, 2), (stage_r, 0), (stage_r, 1), (stage_r, 2),
        (stage_d, 0), (stage_d, 1), (gram_a, 0, 64), (stage_d, 2), (gram_a, 64, 32),
        (stage_f, 0), (stage_f, 1), (stage_f, 2), (gram_b,), (stage_h, 0), (stage_h, 1), (stage_h, 2),
        (gram_c,), (eliminate, 0, 5), (stage_i, 0), (stage_i, 1), (stage_i, 2), (eliminate, 5, 8), (invert,), (gram_d,),
        (stage_k, 0), (stage_k, 1), (stage_k, 2),
    ]
    for stage in plan:
        stage[0](*stage[1:])
    few = r1.at[pl.ds(0, LAYERS), pl.ds(0, 2), pl.ds(0, 3)]
    for n, like in enumerate((p_part, p_part, r1, few, few, r1, gram_y.at[pl.ds(0, 3)], gram_z.at[pl.ds(0, 3)], aug)):
        drain(like, send.at[n])


def rebuild_kernel(
    replicas, merged, basis, w_all, linv, memory_out, rebuilt_out, query_out, qpad, memory_buf, rebuilt_buf, query_buf, sem
):
    def write(src, dst, n):
        pltpu.make_async_copy(src, dst, sem.at[n]).start()

    for l in range(LAYERS):
        for m in range(2):
            inverse = linv[l, m][:, 0:R]
            high = inverse.astype(BF16)
            low = (inverse - high.astype(F32)).astype(BF16)
            qpad[l, m, R - R * m:2 * R - R * m, :] = jnp.zeros((R, KVW), BF16)
            for j in range(4):
                w = w_all[l, m, j]
                q = jnp.dot(high, w, preferred_element_type=F32) + jnp.dot(low, w, preferred_element_type=F32)
                q = q * (1.0 / replicas)
                query_buf[l, m, :, 256 * j:256 * j + 256] = q
                qpad[l, m, R * m:R * m + R, 256 * j:256 * j + 256] = q.astype(BF16)
            write(query_buf.at[l, m], query_out.at[l, m], 0)
            for r in range(0, ROWS, CHUNK):
                rows = slice(r, r + CHUNK)
                at = pl.ds(r, CHUNK)
                rebuilt = jnp.dot(basis[l, rows], qpad[l, m], preferred_element_type=F32)
                rebuilt_buf[l, m, rows] = rebuilt.astype(BF16)
                memory_buf[l, m, rows] = (merged[l, m, rows].astype(F32) - rebuilt).astype(BF16)
                write(rebuilt_buf.at[l, m, at], rebuilt_out.at[l, m, at], 1)
                write(memory_buf.at[l, m, at], memory_out.at[0, l, m, at], 2)
    for n, buffer in enumerate((query_buf, rebuilt_buf, memory_buf)):
        pltpu.make_async_copy(buffer, buffer, sem.at[n]).wait()


def body(gradients, memory, initial_query):
    replicas = lax.axis_size("dp")
    vmem = pl.BlockSpec(memory_space=pltpu.VMEM)
    hbm = pl.BlockSpec(memory_space=pltpu.HBM)
    query_t = jnp.swapaxes(initial_query, 2, 3)
    dma = pltpu.SemaphoreType.DMA
    merged, basis, w_all, linv = pl.pallas_call(
        reduce_kernel,
        name="reduce",
        out_shape=[
            pltpu.VMEM((LAYERS, 2, ROWS, KVW), BF16),
            pltpu.VMEM((LAYERS, ROWS, 2 * R), BF16),
            pltpu.VMEM((LAYERS, 2, 4, R, 256), BF16),
            pltpu.VMEM((LAYERS, 2, R, 2 * R), F32),
        ],
        in_specs=[hbm, hbm, hbm],
        out_specs=[vmem] * 4,
        scratch_shapes=[
            pltpu.VMEM((LAYERS, 2, ROWS, KVW), BF16),
            pltpu.VMEM((LAYERS, 2, ROWS, KVW), BF16),
            pltpu.VMEM((LAYERS, 2, R, KVW), F32),
            pltpu.VMEM((LAYERS, 2, KVW, 2 * R), BF16),
            pltpu.VMEM((LAYERS, ROWS, 2 * R), F32),
            pltpu.VMEM((LAYERS, ROWS, 2 * R), BF16),
            pltpu.VMEM((LAYERS, 7, 64, 2 * R), BF16),
            pltpu.VMEM((LAYERS, ROWS, 2 * R), BF16),
            pltpu.VMEM((LAYERS, 2 * R, ROWS), BF16),
            pltpu.VMEM((LAYERS, 2, 4, R, 256), BF16),
            pltpu.VMEM((LAYERS, 2, 7, 32, 256), BF16),
            pltpu.VMEM((LAYERS, 2, 4, 32, 256), BF16),
            pltpu.VMEM((LAYERS, 2, 4, 32, 256), BF16),
            pltpu.VMEM((4, 96, 2 * R), F32),
            pltpu.VMEM((4, 96, 2 * R), F32),
            pltpu.VMEM((LAYERS, R, 2 * R), F32),
            dma((LAYERS, 2)),
            dma((LAYERS,)),
            dma((9,)),
            dma((LAYERS, 2)),
            dma((LAYERS, 2, 4)),
            dma((3,)),
            dma,
        ],
        compiler_params=pltpu.CompilerParams(collective_id=0, has_side_effects=True, vmem_limit_bytes=54 << 20),
    )(gradients, memory, query_t)

    new_memory, rebuilt, query = pl.pallas_call(
        functools.partial(rebuild_kernel, replicas),
        name="rebuild",
        out_shape=[
            jax.ShapeDtypeStruct((1, LAYERS, 2, ROWS, KVW), BF16),
            jax.ShapeDtypeStruct((LAYERS, 2, ROWS, KVW), BF16),
            jax.ShapeDtypeStruct((LAYERS, 2, R, KVW), F32),
        ],
        in_specs=[vmem] * 4,
        out_specs=[hbm] * 3,
        scratch_shapes=[
            pltpu.VMEM((LAYERS, 2, 2 * R, KVW), BF16),
            pltpu.VMEM((LAYERS, 2, ROWS, KVW), BF16),
            pltpu.VMEM((LAYERS, 2, ROWS, KVW), BF16),
            pltpu.VMEM((LAYERS, 2, R, KVW), F32),
            dma((3,)),
        ],
        compiler_params=pltpu.CompilerParams(vmem_limit_bytes=36 << 20),
    )(merged, basis, w_all, linv)
    return new_memory, rebuilt, jnp.swapaxes(query, 2, 3)


def solution(mesh):
    in_specs = (P("dp", None, None, "tensor", None), P("dp", None, None, "tensor", None), P())
    out_specs = (P("dp", None, None, "tensor", None), P(None, None, "tensor", None), P())
    return jax.shard_map(body, mesh=mesh, in_specs=in_specs, out_specs=out_specs, check_vma=False)
```

```python
import functools

import jax
import jax.numpy as jnp
from jax import lax
from jax.experimental import pallas as pl
from jax.experimental.pallas import tpu as pltpu
from jax.sharding import PartitionSpec as P

MESH = pl.DeviceIdType.MESH
F32 = jnp.float32
BF16 = jnp.bfloat16
LAYERS = 3
ROWS = 512
KVW = 1024
R = 64
CHUNK = 256
DEPTH = 4
NT = (((1,), (1,)), ((), ()))


def reduce_kernel(
    g_hbm, m_hbm, query_hbm,
    merged, basis, w_all, linv,
    g_buf, m_buf, query, qpad, p_own, p_send, p_part, s_full, s_t, w_send, r1, e1, e2, gram_y, gram_z, aug,
    load_sem, query_sem, send, s_recv, w_arrive, gram_recv, linv_recv,
):
    dp = lax.axis_index("dp")
    tensor = lax.axis_index("tensor")
    core = dp % 2
    coord = (dp // 2, tensor // 4, tensor % 4)

    def along(axis, k, other=0):
        c = [coord[0], coord[1], coord[2]]
        c[axis] = (c[axis] + k) % 4
        return (c[0] * 2 + (core + other) % 2, c[1] * 4 + c[2])

    sibling = (dp + 1 - 2 * core, tensor)

    query_loads = [pltpu.make_async_copy(query_hbm.at[l], query.at[l], query_sem.at[l]) for l in range(LAYERS)]
    loads = [
        (
            pltpu.make_async_copy(g_hbm.at[0, l, m], g_buf.at[l, m], load_sem.at[l, m]),
            pltpu.make_async_copy(m_hbm.at[0, l, m], m_buf.at[l, m], load_sem.at[l, m]),
        )
        for l in range(LAYERS)
        for m in range(2)
    ]

    def load(i):
        if i % 2 == 0:
            query_loads[i // 2].start()
        loads[i][0].start()
        loads[i][1].start()

    for i in range(DEPTH):
        load(i)

    barrier = pltpu.get_barrier_semaphore()
    pl.semaphore_signal(barrier, inc=1, device_id=sibling, device_id_type=MESH)
    for axis in range(3):
        for k in (1, 2, 3):
            for other in range(2):
                pl.semaphore_signal(barrier, inc=1, device_id=along(axis, k, other), device_id_type=MESH)

    column = lax.broadcasted_iota(jnp.int32, (KVW, 2 * R), 1)

    def right_factor(l):
        query_loads[l].wait()
        pair = jnp.concatenate([query[l, 0], query[l, 1]], axis=0).astype(BF16).T
        for m in range(2):
            qpad[l, m] = jnp.where((column >= R * m) & (column < R * m + R), pair, jnp.zeros_like(pair))

    def remote(src, dst, send_sem, recv_sem, device):
        c = pltpu.make_async_remote_copy(src, dst, send_sem, recv_sem, device_id=device, device_id_type=MESH)
        c.start()
        return c

    def drain(like, sem):
        pltpu.make_async_copy(like, like, sem).wait()

    partners = [(k, other) for k in (2, 1, 3) for other in range(2)] + [(0, 1)]
    half = ROWS // 2

    def row64(j):
        return pl.ds(pl.multiple_of(j * 64, 64), 64)

    def stage_a(l):
        right_factor(l)
        for m in range(2):
            i = 2 * l + m
            drain(g_buf.at[0], load_sem.at[l, m])
            if i + DEPTH < len(loads):
                load(i + DEPTH)
            for r in range(0, ROWS, CHUNK):
                rows = slice(r, r + CHUNK)
                block = g_buf[l, m, rows] + m_buf[l, m, rows]
                merged[l, m, rows] = block
                part = jnp.dot(block, qpad[l, m], preferred_element_type=F32)
                p_own[l, rows] = part if m == 0 else p_own[l, rows] + part
        p_send[l] = p_own[l].astype(BF16)
        if l == 0:
            pl.semaphore_wait(barrier, 19)
        for n, (k, other) in enumerate(partners):
            owner = (coord[0] + k) % 4 * 2 + (core + other) % 2
            remote(p_send.at[l, row64(owner)], p_part.at[l, n], send.at[0], s_recv.at[l, 0], along(0, k, other))

    def stage_r(l):
        drain(p_part.at[l], s_recv.at[l, 0])
        total = p_send[l, row64(dp), :].astype(F32)
        for n in range(len(partners)):
            total = total + p_part[l, n].astype(F32)
        piece = s_full.at[l, row64(dp)]
        s_full[l, row64(dp), :] = total.astype(BF16)
        for k, other in partners:
            remote(piece, piece, send.at[1], s_recv.at[l, 1], along(0, k, other))

    def stage_d(l):
        drain(p_part.at[l], s_recv.at[l, 1])
        s_t[l] = s_full[l].T
        for m in range(2):
            w = jnp.dot(s_t[l, R * m:R * m + R, :], merged[l, m], preferred_element_type=F32)
            for j in range(4):
                w_send[l, m, j] = w[:, 256 * j:256 * j + 256].astype(BF16)
        for h in range(2):
            axis = axes(l, h)[0]
            for n, (k, other) in enumerate(partners):
                piece = w_send.at[l, (core + other) % 2, (coord[axis] + k) % 4, pl.ds(32 * h, 32)]
                remote(piece, r1.at[l, h, n], send.at[2], w_arrive.at[l, h, 0], along(axis, k, other))

    def axes(l, h):
        return (l + h) % 3, (l + h + 1) % 3, (l + h + 2) % 3

    def exchange(slots, l, h, phase, value):
        axis = axes(l, h)[phase]
        piece = slots.at[l, h, coord[axis]]
        slots[l, h, coord[axis]] = value.astype(BF16)
        for k in (1, 2, 3):
            remote(piece, piece, send.at[2 + phase], w_arrive.at[l, h, phase], along(axis, k))

    def stage_f(l):
        for h in range(2):
            drain(r1.at[l, h], w_arrive.at[l, h, 0])
            total = w_send[l, core, coord[axes(l, h)[0]], 32 * h:32 * h + 32, :].astype(F32)
            for n in range(len(partners)):
                total = total + r1[l, h, n].astype(F32)
            exchange(e1, l, h, 1, total)

    def in_order(slots):
        return ((slots[0].astype(F32) + slots[1].astype(F32)) + slots[2].astype(F32)) + slots[3].astype(F32)

    def stage_h(l):
        for h in range(2):
            drain(r1.at[l, h, pl.ds(0, 3)], w_arrive.at[l, h, 1])
            exchange(e2, l, h, 2, in_order(e1.at[l, h]))

    def stage_i(l):
        for h in range(2):
            drain(r1.at[l, h, pl.ds(0, 3)], w_arrive.at[l, h, 2])
            axis = axes(l, h)[0]
            mine = coord[axis]
            w_all[l, core, mine, 32 * h:32 * h + 32, :] = in_order(e2.at[l, h]).astype(BF16)
            piece = w_all.at[l, core, mine, pl.ds(32 * h, 32)]
            for k, other in partners:
                remote(piece, piece, send.at[5], w_arrive.at[l, h, 3], along(axis, k, other))

    def stage_k(l):
        for h in range(2):
            drain(r1.at[l, h], w_arrive.at[l, h, 3])

    def gram(l):
        mine = s_t[l, pl.ds(pl.multiple_of(R * core, R), R), :]
        return lax.dot_general(mine, mine, NT, preferred_element_type=F32)

    def gram_a(first, rows):
        slot = coord[1]
        if first == 0:
            gram_y[slot, 0:64, :] = jnp.concatenate([gram(0), gram(1)], axis=1)
        else:
            last = gram(2)
            gram_y[slot, 64:96, :] = jnp.concatenate([last[0:32], last[32:64]], axis=1)
        piece = gram_y.at[slot, pl.ds(first, rows)]
        for k in (1, 2, 3):
            remote(piece, piece, send.at[6], gram_recv.at[first // 64], along(1, k))

    def gram_b():
        drain(gram_y.at[pl.ds(0, 3), pl.ds(0, 64)], gram_recv.at[0])
        drain(gram_y.at[pl.ds(0, 3), pl.ds(64, 32)], gram_recv.at[1])
        slot = coord[2]
        gram_z[slot] = ((gram_y[0] + gram_y[1]) + gram_y[2]) + gram_y[3]
        for k in (1, 2, 3):
            remote(gram_z.at[slot], gram_z.at[slot], send.at[7], gram_recv.at[2], along(2, k))

    def gram_c():
        drain(gram_z.at[pl.ds(0, 3)], gram_recv.at[2])
        total = ((gram_z[0] + gram_z[1]) + gram_z[2]) + gram_z[3]
        lane = lax.broadcasted_iota(jnp.int32, (R, 2 * R), 1)
        row = lax.broadcasted_iota(jnp.int32, (R, 2 * R), 0)
        eye = (lane == row + R).astype(F32)
        both, last = total[0:64], total[64:96]
        aug[0] = jnp.where(lane < R, both, eye)
        aug[1] = jnp.where(lane < R, pltpu.roll(both, R, 1), eye)
        aug[2] = jnp.where(lane < R, jnp.concatenate([last, pltpu.roll(last, R, 1)], axis=0), eye)

    def eliminate(first, end):
        row = lax.broadcasted_iota(jnp.int32, (8, 2 * R), 0)
        state = [aug[l, 8 * first:R, :] for l in range(LAYERS)]
        for b in range(first, end):
            top = [a[0:8] for a in state]
            state = [a[8:] for a in state]
            for i in range(0, 8, 2):
                j = 8 * b + i
                for l in range(LAYERS):
                    t = top[l]
                    col, col2 = (jnp.broadcast_to(t[:, n:n + 1], t.shape) for n in (j, j + 1))
                    inverse = 1.0 / col[i:i + 1]
                    first = t[i:i + 1] * inverse
                    u, v = col[i + 1:i + 2] * inverse, col2[i:i + 1] * inverse
                    second = t[i + 1:i + 2] - u * t[i:i + 1]
                    scaled = second / (col2[i + 1:i + 2] - u * col2[i:i + 1])
                    lower = t - col * first - (col2 - col * v) * scaled
                    top[l] = jnp.where(row > i + 1, lower, jnp.where(row == i + 1, second, t))
                    if j < R - 8:
                        t = state[l]
                        col, col2 = (jnp.broadcast_to(t[:, n:n + 1], t.shape) for n in (j, j + 1))
                        state[l] = t - col * first - (col2 - col * v) * scaled
            for l in range(LAYERS):
                aug[l, 8 * b:8 * b + 8, :] = top[l]
        if end < R // 8:
            for l in range(LAYERS):
                aug[l, 8 * end:R, :] = state[l]

    def invert():
        lane = lax.broadcasted_iota(jnp.int32, (R, 2 * R), 1)
        row = lax.broadcasted_iota(jnp.int32, (R, 2 * R), 0)
        for l in range(LAYERS):
            a = aug[l]
            pivots = jnp.sum(jnp.where(lane == row, a, 0.0), axis=1, keepdims=True)
            linv[l, core] = jnp.where(lane < R, pltpu.roll(a, R, 1) * lax.rsqrt(pivots), 0.0)
            remote(linv.at[l, core], linv.at[l, core], send.at[8], linv_recv, sibling)

    def gram_d():
        drain(aug, linv_recv)
        for l in range(LAYERS):
            block = jnp.concatenate([linv[l, 0], pltpu.roll(linv[l, 1], R, 1)], axis=0)
            high = block.astype(BF16)
            low = (block - high.astype(F32)).astype(BF16)
            for h in range(2):
                s = s_full[l, half * h:half * h + half, :]
                out = lax.dot_general(s, high, NT, preferred_element_type=F32)
                out = out + lax.dot_general(s, low, NT, preferred_element_type=F32)
                basis[l, half * h:half * h + half, :] = out.astype(BF16)

    plan = [
        (stage_a, 0), (stage_a, 1), (stage_a, 2), (stage_r, 0), (stage_r, 1), (stage_r, 2),
        (stage_d, 0), (stage_d, 1), (gram_a, 0, 64), (stage_d, 2), (gram_a, 64, 32),
        (stage_f, 0), (stage_f, 1), (stage_f, 2), (gram_b,), (stage_h, 0), (stage_h, 1), (stage_h, 2),
        (gram_c,), (eliminate, 0, 4), (stage_i, 0), (stage_i, 1), (stage_i, 2), (eliminate, 4, 8), (invert,), (gram_d,),
        (stage_k, 0), (stage_k, 1), (stage_k, 2),
    ]
    for stage in plan:
        stage[0](*stage[1:])
    few = r1.at[pl.ds(0, LAYERS), pl.ds(0, 2), pl.ds(0, 3)]
    for n, like in enumerate((p_part, p_part, r1, few, few, r1, gram_y.at[pl.ds(0, 3)], gram_z.at[pl.ds(0, 3)], aug)):
        drain(like, send.at[n])


def rebuild_kernel(
    replicas, merged, basis, w_all, linv, memory_out, rebuilt_out, query_out, qpad, memory_buf, rebuilt_buf, query_buf, sem
):
    def write(src, dst, n):
        pltpu.make_async_copy(src, dst, sem.at[n]).start()

    for l in range(LAYERS):
        for m in range(2):
            inverse = linv[l, m][:, 0:R]
            high = inverse.astype(BF16)
            low = (inverse - high.astype(F32)).astype(BF16)
            qpad[l, m, R - R * m:2 * R - R * m, :] = jnp.zeros((R, KVW), BF16)
            for j in range(4):
                w = w_all[l, m, j]
                q = jnp.dot(high, w, preferred_element_type=F32) + jnp.dot(low, w, preferred_element_type=F32)
                q = q * (1.0 / replicas)
                query_buf[l, m, :, 256 * j:256 * j + 256] = q
                qpad[l, m, R * m:R * m + R, 256 * j:256 * j + 256] = q.astype(BF16)
            write(query_buf.at[l, m], query_out.at[l, m], 0)
            for r in range(0, ROWS, CHUNK):
                rows = slice(r, r + CHUNK)
                at = pl.ds(r, CHUNK)
                rebuilt = jnp.dot(basis[l, rows], qpad[l, m], preferred_element_type=F32)
                rebuilt_buf[l, m, rows] = rebuilt.astype(BF16)
                memory_buf[l, m, rows] = (merged[l, m, rows].astype(F32) - rebuilt).astype(BF16)
                write(rebuilt_buf.at[l, m, at], rebuilt_out.at[l, m, at], 1)
                write(memory_buf.at[l, m, at], memory_out.at[0, l, m, at], 2)
    for n, buffer in enumerate((query_buf, rebuilt_buf, memory_buf)):
        pltpu.make_async_copy(buffer, buffer, sem.at[n]).wait()


def body(gradients, memory, initial_query):
    replicas = lax.axis_size("dp")
    vmem = pl.BlockSpec(memory_space=pltpu.VMEM)
    hbm = pl.BlockSpec(memory_space=pltpu.HBM)
    query_t = jnp.swapaxes(initial_query, 2, 3)
    dma = pltpu.SemaphoreType.DMA
    merged, basis, w_all, linv = pl.pallas_call(
        reduce_kernel,
        name="reduce",
        out_shape=[
            pltpu.VMEM((LAYERS, 2, ROWS, KVW), BF16),
            pltpu.VMEM((LAYERS, ROWS, 2 * R), BF16),
            pltpu.VMEM((LAYERS, 2, 4, R, 256), BF16),
            pltpu.VMEM((LAYERS, 2, R, 2 * R), F32),
        ],
        in_specs=[hbm, hbm, hbm],
        out_specs=[vmem] * 4,
        scratch_shapes=[
            pltpu.VMEM((LAYERS, 2, ROWS, KVW), BF16),
            pltpu.VMEM((LAYERS, 2, ROWS, KVW), BF16),
            pltpu.VMEM((LAYERS, 2, R, KVW), F32),
            pltpu.VMEM((LAYERS, 2, KVW, 2 * R), BF16),
            pltpu.VMEM((LAYERS, ROWS, 2 * R), F32),
            pltpu.VMEM((LAYERS, ROWS, 2 * R), BF16),
            pltpu.VMEM((LAYERS, 7, 64, 2 * R), BF16),
            pltpu.VMEM((LAYERS, ROWS, 2 * R), BF16),
            pltpu.VMEM((LAYERS, 2 * R, ROWS), BF16),
            pltpu.VMEM((LAYERS, 2, 4, R, 256), BF16),
            pltpu.VMEM((LAYERS, 2, 7, 32, 256), BF16),
            pltpu.VMEM((LAYERS, 2, 4, 32, 256), BF16),
            pltpu.VMEM((LAYERS, 2, 4, 32, 256), BF16),
            pltpu.VMEM((4, 96, 2 * R), F32),
            pltpu.VMEM((4, 96, 2 * R), F32),
            pltpu.VMEM((LAYERS, R, 2 * R), F32),
            dma((LAYERS, 2)),
            dma((LAYERS,)),
            dma((9,)),
            dma((LAYERS, 2)),
            dma((LAYERS, 2, 4)),
            dma((3,)),
            dma,
        ],
        compiler_params=pltpu.CompilerParams(collective_id=0, has_side_effects=True, vmem_limit_bytes=54 << 20),
    )(gradients, memory, query_t)

    new_memory, rebuilt, query = pl.pallas_call(
        functools.partial(rebuild_kernel, replicas),
        name="rebuild",
        out_shape=[
            jax.ShapeDtypeStruct((1, LAYERS, 2, ROWS, KVW), BF16),
            jax.ShapeDtypeStruct((LAYERS, 2, ROWS, KVW), BF16),
            jax.ShapeDtypeStruct((LAYERS, 2, R, KVW), F32),
        ],
        in_specs=[vmem] * 4,
        out_specs=[hbm] * 3,
        scratch_shapes=[
            pltpu.VMEM((LAYERS, 2, 2 * R, KVW), BF16),
            pltpu.VMEM((LAYERS, 2, ROWS, KVW), BF16),
            pltpu.VMEM((LAYERS, 2, ROWS, KVW), BF16),
            pltpu.VMEM((LAYERS, 2, R, KVW), F32),
            dma((3,)),
        ],
        compiler_params=pltpu.CompilerParams(vmem_limit_bytes=36 << 20),
    )(merged, basis, w_all, linv)
    return new_memory, rebuilt, jnp.swapaxes(query, 2, 3)


def solution(mesh):
    in_specs = (P("dp", None, None, "tensor", None), P("dp", None, None, "tensor", None), P())
    out_specs = (P("dp", None, None, "tensor", None), P(None, None, "tensor", None), P())
    return jax.shard_map(body, mesh=mesh, in_specs=in_specs, out_specs=out_specs, check_vma=False)
```

```python
import functools

import jax
import jax.numpy as jnp
from jax import lax
from jax.experimental import pallas as pl
from jax.experimental.pallas import tpu as pltpu
from jax.sharding import PartitionSpec as P

MESH = pl.DeviceIdType.MESH
F32 = jnp.float32
BF16 = jnp.bfloat16
LAYERS = 3
ROWS = 512
KVW = 1024
R = 64
CHUNK = 256
DEPTH = 4
ORDERS = (((1, 2, 0), (2, 0, 1)), ((1, 0, 2), (2, 1, 0)), ((0, 1, 2), (2, 0, 1)))
NT = (((1,), (1,)), ((), ()))


def reduce_kernel(
    g_hbm, m_hbm, query_hbm,
    merged, basis, w_all, linv,
    g_buf, m_buf, query, qpad, p_own, p_send, p_part, s_full, s_t, w_send, r1, e1, e2, gram_y, gram_z, aug,
    load_sem, query_sem, send, s_recv, w_arrive, gram_recv, linv_recv,
):
    dp = lax.axis_index("dp")
    tensor = lax.axis_index("tensor")
    core = dp % 2
    coord = (dp // 2, tensor // 4, tensor % 4)

    def along(axis, k, other=0):
        c = [coord[0], coord[1], coord[2]]
        c[axis] = (c[axis] + k) % 4
        return (c[0] * 2 + (core + other) % 2, c[1] * 4 + c[2])

    sibling = (dp + 1 - 2 * core, tensor)

    query_loads = [pltpu.make_async_copy(query_hbm.at[l], query.at[l], query_sem.at[l]) for l in range(LAYERS)]
    loads = [
        (
            pltpu.make_async_copy(g_hbm.at[0, l, m], g_buf.at[l, m], load_sem.at[l, m]),
            pltpu.make_async_copy(m_hbm.at[0, l, m], m_buf.at[l, m], load_sem.at[l, m]),
        )
        for l in range(LAYERS)
        for m in range(2)
    ]

    def load(i):
        if i % 2 == 0:
            query_loads[i // 2].start()
        loads[i][0].start()
        loads[i][1].start()

    for i in range(DEPTH):
        load(i)

    barrier = pltpu.get_barrier_semaphore()
    pl.semaphore_signal(barrier, inc=1, device_id=sibling, device_id_type=MESH)
    for axis in range(3):
        for k in (1, 2, 3):
            for other in range(2):
                pl.semaphore_signal(barrier, inc=1, device_id=along(axis, k, other), device_id_type=MESH)

    column = lax.broadcasted_iota(jnp.int32, (KVW, 2 * R), 1)

    def right_factor(l):
        query_loads[l].wait()
        pair = jnp.concatenate([query[l, 0], query[l, 1]], axis=0).astype(BF16).T
        for m in range(2):
            qpad[l, m] = jnp.where((column >= R * m) & (column < R * m + R), pair, jnp.zeros_like(pair))

    def remote(src, dst, send_sem, recv_sem, device):
        c = pltpu.make_async_remote_copy(src, dst, send_sem, recv_sem, device_id=device, device_id_type=MESH)
        c.start()
        return c

    def drain(like, sem):
        pltpu.make_async_copy(like, like, sem).wait()

    partners = [(k, other) for k in (2, 1, 3) for other in range(2)] + [(0, 1)]
    half = ROWS // 2

    def row64(j):
        return pl.ds(pl.multiple_of(j * 64, 64), 64)

    def stage_a(l):
        right_factor(l)
        for m in range(2):
            i = 2 * l + m
            drain(g_buf.at[0], load_sem.at[l, m])
            if i + DEPTH < len(loads):
                load(i + DEPTH)
            for r in range(0, ROWS, CHUNK):
                rows = slice(r, r + CHUNK)
                block = g_buf[l, m, rows] + m_buf[l, m, rows]
                merged[l, m, rows] = block
                part = jnp.dot(block, qpad[l, m], preferred_element_type=F32)
                p_own[l, rows] = part if m == 0 else p_own[l, rows] + part
        p_send[l] = p_own[l].astype(BF16)
        if l == 0:
            pl.semaphore_wait(barrier, 19)
        for n, (k, other) in enumerate(partners):
            owner = (coord[0] + k) % 4 * 2 + (core + other) % 2
            remote(p_send.at[l, row64(owner)], p_part.at[l, n], send.at[0], s_recv.at[l, 0], along(0, k, other))

    def stage_r(l):
        drain(p_part.at[l], s_recv.at[l, 0])
        total = p_send[l, row64(dp), :].astype(F32)
        for n in range(len(partners)):
            total = total + p_part[l, n].astype(F32)
        piece = s_full.at[l, row64(dp)]
        s_full[l, row64(dp), :] = total.astype(BF16)
        for k, other in partners:
            remote(piece, piece, send.at[1], s_recv.at[l, 1], along(0, k, other))

    def stage_d(l):
        drain(p_part.at[l], s_recv.at[l, 1])
        s_t[l] = s_full[l].T
        for m in range(2):
            w = jnp.dot(s_t[l, R * m:R * m + R, :], merged[l, m], preferred_element_type=F32)
            for j in range(4):
                w_send[l, m, j] = w[:, 256 * j:256 * j + 256].astype(BF16)
        for h in range(2):
            axis = axes(l, h)[0]
            for n, (k, other) in enumerate(partners):
                piece = w_send.at[l, (core + other) % 2, (coord[axis] + k) % 4, pl.ds(32 * h, 32)]
                remote(piece, r1.at[l, h, n], send.at[2], w_arrive.at[l, h, 0], along(axis, k, other))

    def axes(l, h):
        return ORDERS[l][h]

    def exchange(slots, l, h, phase, value):
        axis = axes(l, h)[phase]
        piece = slots.at[l, h, coord[axis]]
        slots[l, h, coord[axis]] = value.astype(BF16)
        for k in (1, 2, 3):
            remote(piece, piece, send.at[2 + phase], w_arrive.at[l, h, phase], along(axis, k))

    def stage_f(l):
        for h in range(2):
            drain(r1.at[l, h], w_arrive.at[l, h, 0])
            total = w_send[l, core, coord[axes(l, h)[0]], 32 * h:32 * h + 32, :].astype(F32)
            for n in range(len(partners)):
                total = total + r1[l, h, n].astype(F32)
            exchange(e1, l, h, 1, total)

    def in_order(slots):
        return ((slots[0].astype(F32) + slots[1].astype(F32)) + slots[2].astype(F32)) + slots[3].astype(F32)

    def stage_h(l):
        for h in range(2):
            drain(r1.at[l, h, pl.ds(0, 3)], w_arrive.at[l, h, 1])
            exchange(e2, l, h, 2, in_order(e1.at[l, h]))

    def stage_i(l):
        for h in range(2):
            drain(r1.at[l, h, pl.ds(0, 3)], w_arrive.at[l, h, 2])
            axis = axes(l, h)[0]
            mine = coord[axis]
            w_all[l, core, mine, 32 * h:32 * h + 32, :] = in_order(e2.at[l, h]).astype(BF16)
            piece = w_all.at[l, core, mine, pl.ds(32 * h, 32)]
            for k, other in partners:
                remote(piece, piece, send.at[5], w_arrive.at[l, h, 3], along(axis, k, other))

    def stage_k(l):
        for h in range(2):
            drain(r1.at[l, h], w_arrive.at[l, h, 3])

    def gram(l):
        mine = s_t[l, pl.ds(pl.multiple_of(R * core, R), R), :]
        return lax.dot_general(mine, mine, NT, preferred_element_type=F32)

    def gram_a(first, rows):
        slot = coord[1]
        if first == 0:
            gram_y[slot, 0:64, :] = jnp.concatenate([gram(0), gram(1)], axis=1)
        else:
            last = gram(2)
            gram_y[slot, 64:96, :] = jnp.concatenate([last[0:32], last[32:64]], axis=1)
        piece = gram_y.at[slot, pl.ds(first, rows)]
        for k in (1, 2, 3):
            remote(piece, piece, send.at[6], gram_recv.at[first // 64], along(1, k))

    def gram_b():
        drain(gram_y.at[pl.ds(0, 3), pl.ds(0, 64)], gram_recv.at[0])
        drain(gram_y.at[pl.ds(0, 3), pl.ds(64, 32)], gram_recv.at[1])
        slot = coord[2]
        gram_z[slot] = ((gram_y[0] + gram_y[1]) + gram_y[2]) + gram_y[3]
        for k in (1, 2, 3):
            remote(gram_z.at[slot], gram_z.at[slot], send.at[7], gram_recv.at[2], along(2, k))

    def gram_c():
        drain(gram_z.at[pl.ds(0, 3)], gram_recv.at[2])
        total = ((gram_z[0] + gram_z[1]) + gram_z[2]) + gram_z[3]
        lane = lax.broadcasted_iota(jnp.int32, (R, 2 * R), 1)
        row = lax.broadcasted_iota(jnp.int32, (R, 2 * R), 0)
        eye = (lane == row + R).astype(F32)
        both, last = total[0:64], total[64:96]
        aug[0] = jnp.where(lane < R, both, eye)
        aug[1] = jnp.where(lane < R, pltpu.roll(both, R, 1), eye)
        aug[2] = jnp.where(lane < R, jnp.concatenate([last, pltpu.roll(last, R, 1)], axis=0), eye)

    def eliminate(first, end):
        row = lax.broadcasted_iota(jnp.int32, (8, 2 * R), 0)
        state = [aug[l, 8 * first:R, :] for l in range(LAYERS)]
        for b in range(first, end):
            top = [a[0:8] for a in state]
            state = [a[8:] for a in state]
            for i in range(0, 8, 2):
                j = 8 * b + i
                for l in range(LAYERS):
                    t = top[l]
                    col, col2 = (jnp.broadcast_to(t[:, n:n + 1], t.shape) for n in (j, j + 1))
                    inverse = 1.0 / col[i:i + 1]
                    first = t[i:i + 1] * inverse
                    u, v = col[i + 1:i + 2] * inverse, col2[i:i + 1] * inverse
                    second = t[i + 1:i + 2] - u * t[i:i + 1]
                    scaled = second / (col2[i + 1:i + 2] - u * col2[i:i + 1])
                    lower = t - col * first - (col2 - col * v) * scaled
                    top[l] = jnp.where(row > i + 1, lower, jnp.where(row == i + 1, second, t))
                    if j < R - 8:
                        t = state[l]
                        col, col2 = (jnp.broadcast_to(t[:, n:n + 1], t.shape) for n in (j, j + 1))
                        state[l] = t - col * first - (col2 - col * v) * scaled
            for l in range(LAYERS):
                aug[l, 8 * b:8 * b + 8, :] = top[l]
        if end < R // 8:
            for l in range(LAYERS):
                aug[l, 8 * end:R, :] = state[l]

    def invert():
        lane = lax.broadcasted_iota(jnp.int32, (R, 2 * R), 1)
        row = lax.broadcasted_iota(jnp.int32, (R, 2 * R), 0)
        for l in range(LAYERS):
            a = aug[l]
            pivots = jnp.sum(jnp.where(lane == row, a, 0.0), axis=1, keepdims=True)
            linv[l, core] = jnp.where(lane < R, pltpu.roll(a, R, 1) * lax.rsqrt(pivots), 0.0)
            remote(linv.at[l, core], linv.at[l, core], send.at[8], linv_recv, sibling)

    def gram_d():
        drain(aug, linv_recv)
        for l in range(LAYERS):
            block = jnp.concatenate([linv[l, 0], pltpu.roll(linv[l, 1], R, 1)], axis=0)
            high = block.astype(BF16)
            low = (block - high.astype(F32)).astype(BF16)
            for h in range(2):
                s = s_full[l, half * h:half * h + half, :]
                out = lax.dot_general(s, high, NT, preferred_element_type=F32)
                out = out + lax.dot_general(s, low, NT, preferred_element_type=F32)
                basis[l, half * h:half * h + half, :] = out.astype(BF16)

    plan = [
        (stage_a, 0), (stage_a, 1), (stage_a, 2), (stage_r, 0), (stage_r, 1), (stage_r, 2),
        (stage_d, 0), (stage_d, 1), (stage_d, 2), (gram_a, 0, 64), (gram_a, 64, 32),
        (stage_f, 0), (stage_f, 1), (stage_f, 2), (gram_b,), (stage_h, 0), (stage_h, 1), (stage_h, 2),
        (gram_c,), (eliminate, 0, 4), (stage_i, 0), (stage_i, 1), (stage_i, 2), (eliminate, 4, 8), (invert,), (gram_d,),
        (stage_k, 0), (stage_k, 1), (stage_k, 2),
    ]
    for stage in plan:
        stage[0](*stage[1:])
    few = r1.at[pl.ds(0, LAYERS), pl.ds(0, 2), pl.ds(0, 3)]
    for n, like in enumerate((p_part, p_part, r1, few, few, r1, gram_y.at[pl.ds(0, 3)], gram_z.at[pl.ds(0, 3)], aug)):
        drain(like, send.at[n])


def rebuild_kernel(
    replicas, merged, basis, w_all, linv, memory_out, rebuilt_out, query_out, qpad, memory_buf, rebuilt_buf, query_buf, sem
):
    def write(src, dst, n):
        pltpu.make_async_copy(src, dst, sem.at[n]).start()

    for l in range(LAYERS):
        for m in range(2):
            inverse = linv[l, m][:, 0:R]
            high = inverse.astype(BF16)
            low = (inverse - high.astype(F32)).astype(BF16)
            qpad[l, m, R - R * m:2 * R - R * m, :] = jnp.zeros((R, KVW), BF16)
            for j in range(4):
                w = w_all[l, m, j]
                q = jnp.dot(high, w, preferred_element_type=F32) + jnp.dot(low, w, preferred_element_type=F32)
                q = q * (1.0 / replicas)
                query_buf[l, m, :, 256 * j:256 * j + 256] = q
                qpad[l, m, R * m:R * m + R, 256 * j:256 * j + 256] = q.astype(BF16)
            write(query_buf.at[l, m], query_out.at[l, m], 0)
            for r in range(0, ROWS, CHUNK):
                rows = slice(r, r + CHUNK)
                at = pl.ds(r, CHUNK)
                rebuilt = jnp.dot(basis[l, rows], qpad[l, m], preferred_element_type=F32)
                rebuilt_buf[l, m, rows] = rebuilt.astype(BF16)
                memory_buf[l, m, rows] = (merged[l, m, rows].astype(F32) - rebuilt).astype(BF16)
                write(rebuilt_buf.at[l, m, at], rebuilt_out.at[l, m, at], 1)
                write(memory_buf.at[l, m, at], memory_out.at[0, l, m, at], 2)
    for n, buffer in enumerate((query_buf, rebuilt_buf, memory_buf)):
        pltpu.make_async_copy(buffer, buffer, sem.at[n]).wait()


def body(gradients, memory, initial_query):
    replicas = lax.axis_size("dp")
    vmem = pl.BlockSpec(memory_space=pltpu.VMEM)
    hbm = pl.BlockSpec(memory_space=pltpu.HBM)
    query_t = jnp.swapaxes(initial_query, 2, 3)
    dma = pltpu.SemaphoreType.DMA
    merged, basis, w_all, linv = pl.pallas_call(
        reduce_kernel,
        name="reduce",
        out_shape=[
            pltpu.VMEM((LAYERS, 2, ROWS, KVW), BF16),
            pltpu.VMEM((LAYERS, ROWS, 2 * R), BF16),
            pltpu.VMEM((LAYERS, 2, 4, R, 256), BF16),
            pltpu.VMEM((LAYERS, 2, R, 2 * R), F32),
        ],
        in_specs=[hbm, hbm, hbm],
        out_specs=[vmem] * 4,
        scratch_shapes=[
            pltpu.VMEM((LAYERS, 2, ROWS, KVW), BF16),
            pltpu.VMEM((LAYERS, 2, ROWS, KVW), BF16),
            pltpu.VMEM((LAYERS, 2, R, KVW), F32),
            pltpu.VMEM((LAYERS, 2, KVW, 2 * R), BF16),
            pltpu.VMEM((LAYERS, ROWS, 2 * R), F32),
            pltpu.VMEM((LAYERS, ROWS, 2 * R), BF16),
            pltpu.VMEM((LAYERS, 7, 64, 2 * R), BF16),
            pltpu.VMEM((LAYERS, ROWS, 2 * R), BF16),
            pltpu.VMEM((LAYERS, 2 * R, ROWS), BF16),
            pltpu.VMEM((LAYERS, 2, 4, R, 256), BF16),
            pltpu.VMEM((LAYERS, 2, 7, 32, 256), BF16),
            pltpu.VMEM((LAYERS, 2, 4, 32, 256), BF16),
            pltpu.VMEM((LAYERS, 2, 4, 32, 256), BF16),
            pltpu.VMEM((4, 96, 2 * R), F32),
            pltpu.VMEM((4, 96, 2 * R), F32),
            pltpu.VMEM((LAYERS, R, 2 * R), F32),
            dma((LAYERS, 2)),
            dma((LAYERS,)),
            dma((9,)),
            dma((LAYERS, 2)),
            dma((LAYERS, 2, 4)),
            dma((3,)),
            dma,
        ],
        compiler_params=pltpu.CompilerParams(collective_id=0, has_side_effects=True, vmem_limit_bytes=54 << 20),
    )(gradients, memory, query_t)

    new_memory, rebuilt, query = pl.pallas_call(
        functools.partial(rebuild_kernel, replicas),
        name="rebuild",
        out_shape=[
            jax.ShapeDtypeStruct((1, LAYERS, 2, ROWS, KVW), BF16),
            jax.ShapeDtypeStruct((LAYERS, 2, ROWS, KVW), BF16),
            jax.ShapeDtypeStruct((LAYERS, 2, R, KVW), F32),
        ],
        in_specs=[vmem] * 4,
        out_specs=[hbm] * 3,
        scratch_shapes=[
            pltpu.VMEM((LAYERS, 2, 2 * R, KVW), BF16),
            pltpu.VMEM((LAYERS, 2, ROWS, KVW), BF16),
            pltpu.VMEM((LAYERS, 2, ROWS, KVW), BF16),
            pltpu.VMEM((LAYERS, 2, R, KVW), F32),
            dma((3,)),
        ],
        compiler_params=pltpu.CompilerParams(vmem_limit_bytes=36 << 20),
    )(merged, basis, w_all, linv)
    return new_memory, rebuilt, jnp.swapaxes(query, 2, 3)


def solution(mesh):
    in_specs = (P("dp", None, None, "tensor", None), P("dp", None, None, "tensor", None), P())
    out_specs = (P("dp", None, None, "tensor", None), P(None, None, "tensor", None), P())
    return jax.shard_map(body, mesh=mesh, in_specs=in_specs, out_specs=out_specs, check_vma=False)
```

```python
import functools

import jax
import jax.numpy as jnp
from jax import lax
from jax.experimental import pallas as pl
from jax.experimental.pallas import tpu as pltpu
from jax.sharding import PartitionSpec as P

MESH = pl.DeviceIdType.MESH
F32 = jnp.float32
BF16 = jnp.bfloat16
LAYERS = 3
ROWS = 512
KVW = 1024
R = 64
CHUNK = 256
DEPTH = 4
ORDERS = (((1, 2, 0), (2, 0, 1)), ((1, 0, 2), (2, 1, 0)), ((0, 1, 2), (2, 0, 1)))
NT = (((1,), (1,)), ((), ()))


def reduce_kernel(
    g_hbm, m_hbm, query_hbm,
    merged, basis, w_all, linv,
    g_buf, m_buf, query, qpad, p_own, p_send, p_part, s_full, s_t, w_send, r1, e1, e2, gram_y, gram_z, aug,
    load_sem, query_sem, send, s_recv, w_arrive, gram_recv, linv_recv,
):
    dp = lax.axis_index("dp")
    tensor = lax.axis_index("tensor")
    core = dp % 2
    coord = (dp // 2, tensor // 4, tensor % 4)

    cores = (core, 1 - core)
    ring = {(axis, k): lax.rem(coord[axis] + k, 4) if k else coord[axis] for axis in range(3) for k in range(4)}
    devices = {}
    for axis in range(3):
        for k in range(4):
            for other in range(2):
                x, y, z = (ring[axis, k] if a == axis else coord[a] for a in range(3))
                devices[axis, k, other] = (x * 2 + cores[other], y * 4 + z)
    sibling = devices[0, 0, 1]

    def along(axis, k, other=0):
        return devices[axis, k, other]

    query_loads = [pltpu.make_async_copy(query_hbm.at[l], query.at[l], query_sem.at[l]) for l in range(LAYERS)]
    loads = [
        (
            pltpu.make_async_copy(g_hbm.at[0, l, m], g_buf.at[l, m], load_sem.at[l, m]),
            pltpu.make_async_copy(m_hbm.at[0, l, m], m_buf.at[l, m], load_sem.at[l, m]),
        )
        for l in range(LAYERS)
        for m in range(2)
    ]

    def load(i):
        if i % 2 == 0:
            query_loads[i // 2].start()
        loads[i][0].start()
        loads[i][1].start()

    for i in range(DEPTH):
        load(i)

    barrier = pltpu.get_barrier_semaphore()
    pl.semaphore_signal(barrier, inc=1, device_id=sibling, device_id_type=MESH)
    for axis in range(3):
        for k in (1, 2, 3):
            for other in range(2):
                pl.semaphore_signal(barrier, inc=1, device_id=along(axis, k, other), device_id_type=MESH)

    column = lax.broadcasted_iota(jnp.int32, (KVW, 2 * R), 1)

    def right_factor(l):
        query_loads[l].wait()
        pair = jnp.concatenate([query[l, 0], query[l, 1]], axis=0).astype(BF16).T
        for m in range(2):
            qpad[l, m] = jnp.where((column >= R * m) & (column < R * m + R), pair, jnp.zeros_like(pair))

    def remote(src, dst, send_sem, recv_sem, device):
        c = pltpu.make_async_remote_copy(src, dst, send_sem, recv_sem, device_id=device, device_id_type=MESH)
        c.start()
        return c

    def drain(like, sem):
        pltpu.make_async_copy(like, like, sem).wait()

    partners = [(k, other) for k in (2, 1, 3) for other in range(2)] + [(0, 1)]
    half = ROWS // 2

    def row64(j):
        return pl.ds(pl.multiple_of(j * 64, 64), 64)

    def stage_a(l):
        right_factor(l)
        for m in range(2):
            i = 2 * l + m
            drain(g_buf.at[0], load_sem.at[l, m])
            if i + DEPTH < len(loads):
                load(i + DEPTH)
            for r in range(0, ROWS, CHUNK):
                rows = slice(r, r + CHUNK)
                block = g_buf[l, m, rows] + m_buf[l, m, rows]
                merged[l, m, rows] = block
                part = jnp.dot(block, qpad[l, m], preferred_element_type=F32)
                p_own[l, rows] = part if m == 0 else p_own[l, rows] + part
        p_send[l] = p_own[l].astype(BF16)
        if l == 0:
            pl.semaphore_wait(barrier, 19)
        for n, (k, other) in enumerate(partners):
            owner = ring[0, k] * 2 + cores[other]
            remote(p_send.at[l, row64(owner)], p_part.at[l, n], send.at[0], s_recv.at[l, 0], along(0, k, other))

    def stage_r(l):
        drain(p_part.at[l], s_recv.at[l, 0])
        total = p_send[l, row64(dp), :].astype(F32)
        for n in range(len(partners)):
            total = total + p_part[l, n].astype(F32)
        piece = s_full.at[l, row64(dp)]
        s_full[l, row64(dp), :] = total.astype(BF16)
        for k, other in partners:
            remote(piece, piece, send.at[1], s_recv.at[l, 1], along(0, k, other))

    def stage_d(l):
        drain(p_part.at[l], s_recv.at[l, 1])
        s_t[l] = s_full[l].T
        for m in range(2):
            w = jnp.dot(s_t[l, R * m:R * m + R, :], merged[l, m], preferred_element_type=F32)
            for j in range(4):
                w_send[l, m, j] = w[:, 256 * j:256 * j + 256].astype(BF16)
        for h in range(2):
            axis = axes(l, h)[0]
            for n, (k, other) in enumerate(partners):
                piece = w_send.at[l, cores[other], ring[axis, k], pl.ds(32 * h, 32)]
                remote(piece, r1.at[l, h, n], send.at[2], w_arrive.at[l, h, 0], along(axis, k, other))

    def axes(l, h):
        return ORDERS[l][h]

    def exchange(slots, l, h, phase, value):
        axis = axes(l, h)[phase]
        piece = slots.at[l, h, coord[axis]]
        slots[l, h, coord[axis]] = value.astype(BF16)
        for k in (1, 2, 3):
            remote(piece, piece, send.at[2 + phase], w_arrive.at[l, h, phase], along(axis, k))

    def stage_f(l):
        for h in range(2):
            drain(r1.at[l, h], w_arrive.at[l, h, 0])
            total = w_send[l, core, coord[axes(l, h)[0]], 32 * h:32 * h + 32, :].astype(F32)
            for n in range(len(partners)):
                total = total + r1[l, h, n].astype(F32)
            exchange(e1, l, h, 1, total)

    def in_order(slots):
        return ((slots[0].astype(F32) + slots[1].astype(F32)) + slots[2].astype(F32)) + slots[3].astype(F32)

    def stage_h(l):
        for h in range(2):
            drain(r1.at[l, h, pl.ds(0, 3)], w_arrive.at[l, h, 1])
            exchange(e2, l, h, 2, in_order(e1.at[l, h]))

    def stage_i(l):
        for h in range(2):
            drain(r1.at[l, h, pl.ds(0, 3)], w_arrive.at[l, h, 2])
            axis = axes(l, h)[0]
            mine = coord[axis]
            w_all[l, core, mine, 32 * h:32 * h + 32, :] = in_order(e2.at[l, h]).astype(BF16)
            piece = w_all.at[l, core, mine, pl.ds(32 * h, 32)]
            for k, other in partners:
                remote(piece, piece, send.at[5], w_arrive.at[l, h, 3], along(axis, k, other))

    def stage_k(l):
        for h in range(2):
            drain(r1.at[l, h], w_arrive.at[l, h, 3])

    def gram(l):
        mine = s_t[l, pl.ds(pl.multiple_of(R * core, R), R), :]
        return lax.dot_general(mine, mine, NT, preferred_element_type=F32)

    def gram_a(first, rows):
        slot = coord[1]
        if first == 0:
            gram_y[slot, 0:64, :] = jnp.concatenate([gram(0), gram(1)], axis=1)
        else:
            last = gram(2)
            gram_y[slot, 64:96, :] = jnp.concatenate([last[0:32], last[32:64]], axis=1)
        piece = gram_y.at[slot, pl.ds(first, rows)]
        for k in (1, 2, 3):
            remote(piece, piece, send.at[6], gram_recv.at[first // 64], along(1, k))

    def gram_b():
        drain(gram_y.at[pl.ds(0, 3), pl.ds(0, 64)], gram_recv.at[0])
        drain(gram_y.at[pl.ds(0, 3), pl.ds(64, 32)], gram_recv.at[1])
        slot = coord[2]
        gram_z[slot] = ((gram_y[0] + gram_y[1]) + gram_y[2]) + gram_y[3]
        for k in (1, 2, 3):
            remote(gram_z.at[slot], gram_z.at[slot], send.at[7], gram_recv.at[2], along(2, k))

    def gram_c():
        drain(gram_z.at[pl.ds(0, 3)], gram_recv.at[2])
        total = ((gram_z[0] + gram_z[1]) + gram_z[2]) + gram_z[3]
        lane = lax.broadcasted_iota(jnp.int32, (R, 2 * R), 1)
        row = lax.broadcasted_iota(jnp.int32, (R, 2 * R), 0)
        eye = (lane == row + R).astype(F32)
        both, last = total[0:64], total[64:96]
        aug[0] = jnp.where(lane < R, both, eye)
        aug[1] = jnp.where(lane < R, pltpu.roll(both, R, 1), eye)
        aug[2] = jnp.where(lane < R, jnp.concatenate([last, pltpu.roll(last, R, 1)], axis=0), eye)

    def eliminate(first, end):
        row = lax.broadcasted_iota(jnp.int32, (8, 2 * R), 0)
        state = [aug[l, 8 * first:R, :] for l in range(LAYERS)]
        for b in range(first, end):
            top = [a[0:8] for a in state]
            state = [a[8:] for a in state]
            for i in range(0, 8, 2):
                j = 8 * b + i
                for l in range(LAYERS):
                    t = top[l]
                    col, col2 = (jnp.broadcast_to(t[:, n:n + 1], t.shape) for n in (j, j + 1))
                    inverse = 1.0 / col[i:i + 1]
                    first = t[i:i + 1] * inverse
                    u, v = col[i + 1:i + 2] * inverse, col2[i:i + 1] * inverse
                    second = t[i + 1:i + 2] - u * t[i:i + 1]
                    scaled = second / (col2[i + 1:i + 2] - u * col2[i:i + 1])
                    lower = t - col * first - (col2 - col * v) * scaled
                    top[l] = jnp.where(row > i + 1, lower, jnp.where(row == i + 1, second, t))
                    if j < R - 8:
                        t = state[l]
                        col, col2 = (jnp.broadcast_to(t[:, n:n + 1], t.shape) for n in (j, j + 1))
                        state[l] = t - col * first - (col2 - col * v) * scaled
            for l in range(LAYERS):
                aug[l, 8 * b:8 * b + 8, :] = top[l]
        if end < R // 8:
            for l in range(LAYERS):
                aug[l, 8 * end:R, :] = state[l]

    def invert():
        lane = lax.broadcasted_iota(jnp.int32, (R, 2 * R), 1)
        row = lax.broadcasted_iota(jnp.int32, (R, 2 * R), 0)
        for l in range(LAYERS):
            a = aug[l]
            pivots = jnp.sum(jnp.where(lane == row, a, 0.0), axis=1, keepdims=True)
            linv[l, core] = jnp.where(lane < R, pltpu.roll(a, R, 1) * lax.rsqrt(pivots), 0.0)
            remote(linv.at[l, core], linv.at[l, core], send.at[8], linv_recv, sibling)

    def gram_d():
        drain(aug, linv_recv)
        for l in range(LAYERS):
            block = jnp.concatenate([linv[l, 0], pltpu.roll(linv[l, 1], R, 1)], axis=0)
            high = block.astype(BF16)
            low = (block - high.astype(F32)).astype(BF16)
            for h in range(2):
                s = s_full[l, half * h:half * h + half, :]
                out = lax.dot_general(s, high, NT, preferred_element_type=F32)
                out = out + lax.dot_general(s, low, NT, preferred_element_type=F32)
                basis[l, half * h:half * h + half, :] = out.astype(BF16)

    plan = [
        (stage_a, 0), (stage_a, 1), (stage_a, 2), (stage_r, 0), (stage_r, 1), (stage_r, 2),
        (stage_d, 0), (stage_d, 1), (stage_d, 2), (gram_a, 0, 64), (gram_a, 64, 32),
        (stage_f, 0), (stage_f, 1), (stage_f, 2), (gram_b,), (stage_h, 0), (stage_h, 1), (stage_h, 2),
        (gram_c,), (eliminate, 0, 4), (stage_i, 0), (stage_i, 1), (stage_i, 2), (eliminate, 4, 8), (invert,), (gram_d,),
        (stage_k, 0), (stage_k, 1), (stage_k, 2),
    ]
    for stage in plan:
        stage[0](*stage[1:])
    few = r1.at[pl.ds(0, LAYERS), pl.ds(0, 2), pl.ds(0, 3)]
    for n, like in enumerate((p_part, p_part, r1, few, few, r1, gram_y.at[pl.ds(0, 3)], gram_z.at[pl.ds(0, 3)], aug)):
        drain(like, send.at[n])


def rebuild_kernel(
    replicas, merged, basis, w_all, linv, memory_out, rebuilt_out, query_out, qpad, memory_buf, rebuilt_buf, query_buf, sem
):
    def write(src, dst, n):
        pltpu.make_async_copy(src, dst, sem.at[n]).start()

    for l in range(LAYERS):
        for m in range(2):
            inverse = linv[l, m][:, 0:R]
            high = inverse.astype(BF16)
            low = (inverse - high.astype(F32)).astype(BF16)
            qpad[l, m, R - R * m:2 * R - R * m, :] = jnp.zeros((R, KVW), BF16)
            for j in range(4):
                w = w_all[l, m, j]
                q = jnp.dot(high, w, preferred_element_type=F32) + jnp.dot(low, w, preferred_element_type=F32)
                q = q * (1.0 / replicas)
                query_buf[l, m, :, 256 * j:256 * j + 256] = q
                qpad[l, m, R * m:R * m + R, 256 * j:256 * j + 256] = q.astype(BF16)
            write(query_buf.at[l, m], query_out.at[l, m], 0)
            for r in range(0, ROWS, CHUNK):
                rows = slice(r, r + CHUNK)
                at = pl.ds(r, CHUNK)
                rebuilt = jnp.dot(basis[l, rows], qpad[l, m], preferred_element_type=F32)
                rebuilt_buf[l, m, rows] = rebuilt.astype(BF16)
                memory_buf[l, m, rows] = (merged[l, m, rows].astype(F32) - rebuilt).astype(BF16)
                write(rebuilt_buf.at[l, m, at], rebuilt_out.at[l, m, at], 1)
                write(memory_buf.at[l, m, at], memory_out.at[0, l, m, at], 2)
    for n, buffer in enumerate((query_buf, rebuilt_buf, memory_buf)):
        pltpu.make_async_copy(buffer, buffer, sem.at[n]).wait()


def body(gradients, memory, initial_query):
    replicas = lax.axis_size("dp")
    vmem = pl.BlockSpec(memory_space=pltpu.VMEM)
    hbm = pl.BlockSpec(memory_space=pltpu.HBM)
    query_t = jnp.swapaxes(initial_query, 2, 3)
    dma = pltpu.SemaphoreType.DMA
    merged, basis, w_all, linv = pl.pallas_call(
        reduce_kernel,
        name="reduce",
        out_shape=[
            pltpu.VMEM((LAYERS, 2, ROWS, KVW), BF16),
            pltpu.VMEM((LAYERS, ROWS, 2 * R), BF16),
            pltpu.VMEM((LAYERS, 2, 4, R, 256), BF16),
            pltpu.VMEM((LAYERS, 2, R, 2 * R), F32),
        ],
        in_specs=[hbm, hbm, hbm],
        out_specs=[vmem] * 4,
        scratch_shapes=[
            pltpu.VMEM((LAYERS, 2, ROWS, KVW), BF16),
            pltpu.VMEM((LAYERS, 2, ROWS, KVW), BF16),
            pltpu.VMEM((LAYERS, 2, R, KVW), F32),
            pltpu.VMEM((LAYERS, 2, KVW, 2 * R), BF16),
            pltpu.VMEM((LAYERS, ROWS, 2 * R), F32),
            pltpu.VMEM((LAYERS, ROWS, 2 * R), BF16),
            pltpu.VMEM((LAYERS, 7, 64, 2 * R), BF16),
            pltpu.VMEM((LAYERS, ROWS, 2 * R), BF16),
            pltpu.VMEM((LAYERS, 2 * R, ROWS), BF16),
            pltpu.VMEM((LAYERS, 2, 4, R, 256), BF16),
            pltpu.VMEM((LAYERS, 2, 7, 32, 256), BF16),
            pltpu.VMEM((LAYERS, 2, 4, 32, 256), BF16),
            pltpu.VMEM((LAYERS, 2, 4, 32, 256), BF16),
            pltpu.VMEM((4, 96, 2 * R), F32),
            pltpu.VMEM((4, 96, 2 * R), F32),
            pltpu.VMEM((LAYERS, R, 2 * R), F32),
            dma((LAYERS, 2)),
            dma((LAYERS,)),
            dma((9,)),
            dma((LAYERS, 2)),
            dma((LAYERS, 2, 4)),
            dma((3,)),
            dma,
        ],
        compiler_params=pltpu.CompilerParams(collective_id=0, has_side_effects=True, vmem_limit_bytes=54 << 20),
    )(gradients, memory, query_t)

    new_memory, rebuilt, query = pl.pallas_call(
        functools.partial(rebuild_kernel, replicas),
        name="rebuild",
        out_shape=[
            jax.ShapeDtypeStruct((1, LAYERS, 2, ROWS, KVW), BF16),
            jax.ShapeDtypeStruct((LAYERS, 2, ROWS, KVW), BF16),
            jax.ShapeDtypeStruct((LAYERS, 2, R, KVW), F32),
        ],
        in_specs=[vmem] * 4,
        out_specs=[hbm] * 3,
        scratch_shapes=[
            pltpu.VMEM((LAYERS, 2, 2 * R, KVW), BF16),
            pltpu.VMEM((LAYERS, 2, ROWS, KVW), BF16),
            pltpu.VMEM((LAYERS, 2, ROWS, KVW), BF16),
            pltpu.VMEM((LAYERS, 2, R, KVW), F32),
            dma((3,)),
        ],
        compiler_params=pltpu.CompilerParams(vmem_limit_bytes=36 << 20),
    )(merged, basis, w_all, linv)
    return new_memory, rebuilt, jnp.swapaxes(query, 2, 3)


def solution(mesh):
    in_specs = (P("dp", None, None, "tensor", None), P("dp", None, None, "tensor", None), P())
    out_specs = (P("dp", None, None, "tensor", None), P(None, None, "tensor", None), P())
    return jax.shard_map(body, mesh=mesh, in_specs=in_specs, out_specs=out_specs, check_vma=False)
```

```python
import functools

import jax
import jax.numpy as jnp
from jax import lax
from jax.experimental import pallas as pl
from jax.experimental.pallas import tpu as pltpu
from jax.sharding import PartitionSpec as P

MESH = pl.DeviceIdType.MESH
F32 = jnp.float32
BF16 = jnp.bfloat16
LAYERS = 3
ROWS = 512
KVW = 1024
R = 64
CHUNK = 256
DEPTH = 3
ORDERS = (((1, 2, 0), (2, 0, 1)), ((1, 0, 2), (2, 1, 0)), ((0, 1, 2), (2, 0, 1)))
NT = (((1,), (1,)), ((), ()))


def reduce_kernel(
    g_hbm, m_hbm, query_hbm,
    merged, basis, w_all, linv,
    g_buf, m_buf, query, qpad, p_own, p_send, p_part, s_full, s_t, w_send, r1, e1, e2, gram_y, gram_z, aug,
    load_sem, query_sem, send, s_recv, w_arrive, gram_recv, linv_recv,
):
    dp = lax.axis_index("dp")
    tensor = lax.axis_index("tensor")
    core = dp % 2
    coord = (dp // 2, tensor // 4, tensor % 4)

    cores = (core, 1 - core)
    ring = {(axis, k): lax.rem(coord[axis] + k, 4) if k else coord[axis] for axis in range(3) for k in range(4)}
    devices = {}
    for axis in range(3):
        for k in range(4):
            for other in range(2):
                x, y, z = (ring[axis, k] if a == axis else coord[a] for a in range(3))
                devices[axis, k, other] = (x * 2 + cores[other], y * 4 + z)
    sibling = devices[0, 0, 1]

    def along(axis, k, other=0):
        return devices[axis, k, other]

    query_loads = [pltpu.make_async_copy(query_hbm.at[l], query.at[l], query_sem.at[l]) for l in range(LAYERS)]
    def load(i):
        l, m = i // 2, i % 2
        if m == 0:
            query_loads[l].start()
        for n in range(ROWS // CHUNK):
            rows = pl.ds(n * CHUNK, CHUNK)
            pltpu.make_async_copy(g_hbm.at[0, l, m, rows], g_buf.at[l, m, rows], load_sem.at[l, m, n]).start()
            pltpu.make_async_copy(m_hbm.at[0, l, m, rows], m_buf.at[l, m, rows], load_sem.at[l, m, n]).start()

    for i in range(DEPTH):
        load(i)

    barrier = pltpu.get_barrier_semaphore()
    pl.semaphore_signal(barrier, inc=1, device_id=sibling, device_id_type=MESH)
    for axis in range(3):
        for k in (1, 2, 3):
            for other in range(2):
                pl.semaphore_signal(barrier, inc=1, device_id=along(axis, k, other), device_id_type=MESH)

    column = lax.broadcasted_iota(jnp.int32, (KVW, 2 * R), 1)

    def right_factor(l):
        query_loads[l].wait()
        pair = jnp.concatenate([query[l, 0], query[l, 1]], axis=0).astype(BF16).T
        for m in range(2):
            qpad[l, m] = jnp.where((column >= R * m) & (column < R * m + R), pair, jnp.zeros_like(pair))

    def remote(src, dst, send_sem, recv_sem, device):
        c = pltpu.make_async_remote_copy(src, dst, send_sem, recv_sem, device_id=device, device_id_type=MESH)
        c.start()
        return c

    def drain(like, sem):
        pltpu.make_async_copy(like, like, sem).wait()

    partners = [(k, other) for k in (2, 1, 3) for other in range(2)] + [(0, 1)]
    half = ROWS // 2

    def row64(j):
        return pl.ds(pl.multiple_of(j * 64, 64), 64)

    def stage_a(l):
        right_factor(l)
        for m in range(2):
            i = 2 * l + m
            if i + DEPTH < 2 * LAYERS:
                load(i + DEPTH)
            for n in range(ROWS // CHUNK):
                drain(g_buf.at[0, :, pl.ds(0, CHUNK)], load_sem.at[l, m, n])
                rows = slice(n * CHUNK, n * CHUNK + CHUNK)
                block = g_buf[l, m, rows] + m_buf[l, m, rows]
                merged[l, m, rows] = block
                part = jnp.dot(block, qpad[l, m], preferred_element_type=F32)
                p_own[l, rows] = part if m == 0 else p_own[l, rows] + part
        p_send[l] = p_own[l].astype(BF16)
        if l == 0:
            pl.semaphore_wait(barrier, 19)
        for n, (k, other) in enumerate(partners):
            owner = ring[0, k] * 2 + cores[other]
            remote(p_send.at[l, row64(owner)], p_part.at[l, n], send.at[0], s_recv.at[l, 0], along(0, k, other))

    def stage_r(l):
        drain(p_part.at[l], s_recv.at[l, 0])
        total = p_send[l, row64(dp), :].astype(F32)
        for n in range(len(partners)):
            total = total + p_part[l, n].astype(F32)
        piece = s_full.at[l, row64(dp)]
        s_full[l, row64(dp), :] = total.astype(BF16)
        for k, other in partners:
            remote(piece, piece, send.at[1], s_recv.at[l, 1], along(0, k, other))

    def stage_d(l):
        drain(p_part.at[l], s_recv.at[l, 1])
        s_t[l] = s_full[l].T
        for m in range(2):
            w = jnp.dot(s_t[l, R * m:R * m + R, :], merged[l, m], preferred_element_type=F32)
            for j in range(4):
                w_send[l, m, j] = w[:, 256 * j:256 * j + 256].astype(BF16)
        for n, (k, other) in enumerate(partners):
            for h in range(2):
                axis = axes(l, h)[0]
                piece = w_send.at[l, cores[other], ring[axis, k], pl.ds(32 * h, 32)]
                remote(piece, r1.at[l, h, n], send.at[2], w_arrive.at[l, h, 0], along(axis, k, other))

    def axes(l, h):
        return ORDERS[l][h]

    def exchange(slots, l, h, phase, value):
        axis = axes(l, h)[phase]
        piece = slots.at[l, h, coord[axis]]
        slots[l, h, coord[axis]] = value.astype(BF16)
        for k in (1, 2, 3):
            remote(piece, piece, send.at[2 + phase], w_arrive.at[l, h, phase], along(axis, k))

    def stage_f(l):
        for h in range(2):
            drain(r1.at[l, h], w_arrive.at[l, h, 0])
            total = w_send[l, core, coord[axes(l, h)[0]], 32 * h:32 * h + 32, :].astype(F32)
            for n in range(len(partners)):
                total = total + r1[l, h, n].astype(F32)
            exchange(e1, l, h, 1, total)

    def in_order(slots):
        return ((slots[0].astype(F32) + slots[1].astype(F32)) + slots[2].astype(F32)) + slots[3].astype(F32)

    def stage_h(l):
        for h in range(2):
            drain(r1.at[l, h, pl.ds(0, 3)], w_arrive.at[l, h, 1])
            exchange(e2, l, h, 2, in_order(e1.at[l, h]))

    def stage_i(l):
        for h in range(2):
            drain(r1.at[l, h, pl.ds(0, 3)], w_arrive.at[l, h, 2])
            axis = axes(l, h)[0]
            mine = coord[axis]
            w_all[l, core, mine, 32 * h:32 * h + 32, :] = in_order(e2.at[l, h]).astype(BF16)
            piece = w_all.at[l, core, mine, pl.ds(32 * h, 32)]
            for k, other in partners:
                remote(piece, piece, send.at[5], w_arrive.at[l, h, 3], along(axis, k, other))

    def stage_k(l):
        for h in range(2):
            drain(r1.at[l, h], w_arrive.at[l, h, 3])

    def gram(l):
        mine = s_t[l, pl.ds(pl.multiple_of(R * core, R), R), :]
        return lax.dot_general(mine, mine, NT, preferred_element_type=F32)

    def gram_a(first, rows):
        slot = coord[1]
        if first == 0:
            gram_y[slot, 0:64, :] = jnp.concatenate([gram(0), gram(1)], axis=1)
        else:
            last = gram(2)
            gram_y[slot, 64:96, :] = jnp.concatenate([last[0:32], last[32:64]], axis=1)
        piece = gram_y.at[slot, pl.ds(first, rows)]
        for k in (1, 2, 3):
            remote(piece, piece, send.at[6], gram_recv.at[first // 64], along(1, k))

    def gram_b():
        drain(gram_y.at[pl.ds(0, 3), pl.ds(0, 64)], gram_recv.at[0])
        drain(gram_y.at[pl.ds(0, 3), pl.ds(64, 32)], gram_recv.at[1])
        slot = coord[2]
        gram_z[slot] = ((gram_y[0] + gram_y[1]) + gram_y[2]) + gram_y[3]
        for k in (1, 2, 3):
            remote(gram_z.at[slot], gram_z.at[slot], send.at[7], gram_recv.at[2], along(2, k))

    def gram_c():
        drain(gram_z.at[pl.ds(0, 3)], gram_recv.at[2])
        total = ((gram_z[0] + gram_z[1]) + gram_z[2]) + gram_z[3]
        lane = lax.broadcasted_iota(jnp.int32, (R, 2 * R), 1)
        row = lax.broadcasted_iota(jnp.int32, (R, 2 * R), 0)
        eye = (lane == row + R).astype(F32)
        both, last = total[0:64], total[64:96]
        aug[0] = jnp.where(lane < R, both, eye)
        aug[1] = jnp.where(lane < R, pltpu.roll(both, R, 1), eye)
        aug[2] = jnp.where(lane < R, jnp.concatenate([last, pltpu.roll(last, R, 1)], axis=0), eye)

    def eliminate(first, end):
        row = lax.broadcasted_iota(jnp.int32, (8, 2 * R), 0)
        state = [aug[l, 8 * first:R, :] for l in range(LAYERS)]
        for b in range(first, end):
            top = [a[0:8] for a in state]
            state = [a[8:] for a in state]
            for i in range(0, 8, 2):
                j = 8 * b + i
                for l in range(LAYERS):
                    t = top[l]
                    col, col2 = (jnp.broadcast_to(t[:, n:n + 1], t.shape) for n in (j, j + 1))
                    inverse = 1.0 / col[i:i + 1]
                    first = t[i:i + 1] * inverse
                    u, v = col[i + 1:i + 2] * inverse, col2[i:i + 1] * inverse
                    second = t[i + 1:i + 2] - u * t[i:i + 1]
                    scaled = second / (col2[i + 1:i + 2] - u * col2[i:i + 1])
                    lower = t - col * first - (col2 - col * v) * scaled
                    top[l] = jnp.where(row > i + 1, lower, jnp.where(row == i + 1, second, t))
                    if j < R - 8:
                        t = state[l]
                        col, col2 = (jnp.broadcast_to(t[:, n:n + 1], t.shape) for n in (j, j + 1))
                        state[l] = t - col * first - (col2 - col * v) * scaled
            for l in range(LAYERS):
                aug[l, 8 * b:8 * b + 8, :] = top[l]
        if end < R // 8:
            for l in range(LAYERS):
                aug[l, 8 * end:R, :] = state[l]

    def invert():
        lane = lax.broadcasted_iota(jnp.int32, (R, 2 * R), 1)
        row = lax.broadcasted_iota(jnp.int32, (R, 2 * R), 0)
        for l in range(LAYERS):
            a = aug[l]
            pivots = jnp.sum(jnp.where(lane == row, a, 0.0), axis=1, keepdims=True)
            linv[l, core] = jnp.where(lane < R, pltpu.roll(a, R, 1) * lax.rsqrt(pivots), 0.0)
            remote(linv.at[l, core], linv.at[l, core], send.at[8], linv_recv, sibling)

    def gram_d():
        drain(aug, linv_recv)
        for l in range(LAYERS):
            block = jnp.concatenate([linv[l, 0], pltpu.roll(linv[l, 1], R, 1)], axis=0)
            high = block.astype(BF16)
            low = (block - high.astype(F32)).astype(BF16)
            for h in range(2):
                s = s_full[l, half * h:half * h + half, :]
                out = lax.dot_general(s, high, NT, preferred_element_type=F32)
                out = out + lax.dot_general(s, low, NT, preferred_element_type=F32)
                basis[l, half * h:half * h + half, :] = out.astype(BF16)

    plan = [
        (stage_a, 0), (stage_a, 1), (stage_a, 2), (stage_r, 0), (stage_r, 1), (stage_r, 2),
        (stage_d, 0), (stage_d, 1), (stage_d, 2), (gram_a, 0, 64), (gram_a, 64, 32),
        (stage_f, 0), (stage_f, 1), (stage_f, 2), (gram_b,), (stage_h, 0), (stage_h, 1), (stage_h, 2),
        (gram_c,), (eliminate, 0, 4), (stage_i, 0), (stage_i, 1), (stage_i, 2), (eliminate, 4, 8), (invert,), (gram_d,),
        (stage_k, 0), (stage_k, 1), (stage_k, 2),
    ]
    for stage in plan:
        stage[0](*stage[1:])
    few = r1.at[pl.ds(0, LAYERS), pl.ds(0, 2), pl.ds(0, 3)]
    for n, like in enumerate((p_part, p_part, r1, few, few, r1, gram_y.at[pl.ds(0, 3)], gram_z.at[pl.ds(0, 3)], aug)):
        drain(like, send.at[n])


def rebuild_kernel(
    replicas, merged, basis, w_all, linv, memory_out, rebuilt_out, query_out, qpad, memory_buf, rebuilt_buf, query_buf, sem
):
    def write(src, dst, n):
        pltpu.make_async_copy(src, dst, sem.at[n]).start()

    for l in range(LAYERS):
        for m in range(2):
            inverse = linv[l, m][:, 0:R]
            high = inverse.astype(BF16)
            low = (inverse - high.astype(F32)).astype(BF16)
            qpad[l, m, R - R * m:2 * R - R * m, :] = jnp.zeros((R, KVW), BF16)
            for j in range(4):
                w = w_all[l, m, j]
                q = jnp.dot(high, w, preferred_element_type=F32) + jnp.dot(low, w, preferred_element_type=F32)
                q = q * (1.0 / replicas)
                query_buf[l, m, :, 256 * j:256 * j + 256] = q
                qpad[l, m, R * m:R * m + R, 256 * j:256 * j + 256] = q.astype(BF16)
            write(query_buf.at[l, m], query_out.at[l, m], 0)
            for r in range(0, ROWS, CHUNK):
                rows = slice(r, r + CHUNK)
                at = pl.ds(r, CHUNK)
                rebuilt = jnp.dot(basis[l, rows], qpad[l, m], preferred_element_type=F32)
                rebuilt_buf[l, m, rows] = rebuilt.astype(BF16)
                memory_buf[l, m, rows] = (merged[l, m, rows].astype(F32) - rebuilt).astype(BF16)
                write(rebuilt_buf.at[l, m, at], rebuilt_out.at[l, m, at], 1)
                write(memory_buf.at[l, m, at], memory_out.at[0, l, m, at], 2)
    for n, buffer in enumerate((query_buf, rebuilt_buf, memory_buf)):
        pltpu.make_async_copy(buffer, buffer, sem.at[n]).wait()


def body(gradients, memory, initial_query):
    replicas = lax.axis_size("dp")
    vmem = pl.BlockSpec(memory_space=pltpu.VMEM)
    hbm = pl.BlockSpec(memory_space=pltpu.HBM)
    query_t = jnp.swapaxes(initial_query, 2, 3)
    dma = pltpu.SemaphoreType.DMA
    merged, basis, w_all, linv = pl.pallas_call(
        reduce_kernel,
        name="reduce",
        out_shape=[
            pltpu.VMEM((LAYERS, 2, ROWS, KVW), BF16),
            pltpu.VMEM((LAYERS, ROWS, 2 * R), BF16),
            pltpu.VMEM((LAYERS, 2, 4, R, 256), BF16),
            pltpu.VMEM((LAYERS, 2, R, 2 * R), F32),
        ],
        in_specs=[hbm, hbm, hbm],
        out_specs=[vmem] * 4,
        scratch_shapes=[
            pltpu.VMEM((LAYERS, 2, ROWS, KVW), BF16),
            pltpu.VMEM((LAYERS, 2, ROWS, KVW), BF16),
            pltpu.VMEM((LAYERS, 2, R, KVW), F32),
            pltpu.VMEM((LAYERS, 2, KVW, 2 * R), BF16),
            pltpu.VMEM((LAYERS, ROWS, 2 * R), F32),
            pltpu.VMEM((LAYERS, ROWS, 2 * R), BF16),
            pltpu.VMEM((LAYERS, 7, 64, 2 * R), BF16),
            pltpu.VMEM((LAYERS, ROWS, 2 * R), BF16),
            pltpu.VMEM((LAYERS, 2 * R, ROWS), BF16),
            pltpu.VMEM((LAYERS, 2, 4, R, 256), BF16),
            pltpu.VMEM((LAYERS, 2, 7, 32, 256), BF16),
            pltpu.VMEM((LAYERS, 2, 4, 32, 256), BF16),
            pltpu.VMEM((LAYERS, 2, 4, 32, 256), BF16),
            pltpu.VMEM((4, 96, 2 * R), F32),
            pltpu.VMEM((4, 96, 2 * R), F32),
            pltpu.VMEM((LAYERS, R, 2 * R), F32),
            dma((LAYERS, 2, ROWS // CHUNK)),
            dma((LAYERS,)),
            dma((9,)),
            dma((LAYERS, 2)),
            dma((LAYERS, 2, 4)),
            dma((3,)),
            dma,
        ],
        compiler_params=pltpu.CompilerParams(collective_id=0, has_side_effects=True, vmem_limit_bytes=54 << 20),
    )(gradients, memory, query_t)

    new_memory, rebuilt, query = pl.pallas_call(
        functools.partial(rebuild_kernel, replicas),
        name="rebuild",
        out_shape=[
            jax.ShapeDtypeStruct((1, LAYERS, 2, ROWS, KVW), BF16),
            jax.ShapeDtypeStruct((LAYERS, 2, ROWS, KVW), BF16),
            jax.ShapeDtypeStruct((LAYERS, 2, R, KVW), F32),
        ],
        in_specs=[vmem] * 4,
        out_specs=[hbm] * 3,
        scratch_shapes=[
            pltpu.VMEM((LAYERS, 2, 2 * R, KVW), BF16),
            pltpu.VMEM((LAYERS, 2, ROWS, KVW), BF16),
            pltpu.VMEM((LAYERS, 2, ROWS, KVW), BF16),
            pltpu.VMEM((LAYERS, 2, R, KVW), F32),
            dma((3,)),
        ],
        compiler_params=pltpu.CompilerParams(vmem_limit_bytes=36 << 20),
    )(merged, basis, w_all, linv)
    return new_memory, rebuilt, jnp.swapaxes(query, 2, 3)


def solution(mesh):
    in_specs = (P("dp", None, None, "tensor", None), P("dp", None, None, "tensor", None), P())
    out_specs = (P("dp", None, None, "tensor", None), P(None, None, "tensor", None), P())
    return jax.shard_map(body, mesh=mesh, in_specs=in_specs, out_specs=out_specs, check_vma=False)
```
